512 devices in a mesh: seq: 16 (over x, y), dp: 32 (over z, core).
Axes of the slice: x: 4, y: 4, z: 16, core: 2. Of those that a mesh axis runs over, the one named last changes fastest.
Arguments:
- signal: bfloat16 [32, 4096, 128], P('dp', 'seq'), may hold values from -6 to 6
- out_grad: bfloat16 [32, 4096, 128], P('dp', 'seq'), may hold values from -6 to 6
- filt: float32 [4096, 128], P('seq'), may hold values from -1.1 to 1.1, as said below
- skip: float32 [128], replicated, may hold values from 0.5 to 1.5
Outputs:
- in_grad: bfloat16 [32, 4096, 128], P('dp', 'seq')
- filt_grad: float32 [4096, 128], P(('seq', 'dp'))
The draws below stay inside these ranges and needn't reach their ends.
Inputs may be any that keep to these rules, and one draw needn't show every extreme that they name: `filt`: each channel's filter is an independent real sequence.
All inputs are finite; a program needn't handle non-finite values.
Results may differ from the reference program's by a relative error of at most 0.001.
Values may be sent and summed in bfloat16 or wider, within the bound.
A program may use at most 64 MiB of HBM per device.

```python
import math
import jax
import jax.numpy as jnp
from jax import lax

CH = 128
SEQS = 32
LENGTH = 4096


def draw_filt(key, part):
    key = jax.random.fold_in(key, 7)
    key_flag, key_slow, key_fast, key_noise = jax.random.split(key, 4)
    slow_flag = jax.random.randint(key_flag, (CH,), 0, 2).astype(jnp.float32)
    slow_rate = jnp.exp(jax.random.uniform(key_slow, (CH,), jnp.float32, jnp.log(0.05 / LENGTH), jnp.log(1.5 / LENGTH)))
    fast_rate = jnp.exp(jax.random.uniform(key_fast, (CH,), jnp.float32, jnp.log(1.0 / 50.0), jnp.log(1.0 / 30.0)))
    rates = slow_flag * slow_rate + (1.0 - slow_flag) * fast_rate
    places = jnp.arange(LENGTH, dtype=jnp.float32)[:, None]
    envelope = jnp.exp(-rates[None, :] * places)
    energy = (1.0 - jnp.exp(-2.0 * rates * LENGTH)) / (1.0 - jnp.exp(-2.0 * rates))
    noise = jnp.clip(jax.random.normal(key_noise, (LENGTH, CH), jnp.float32), -4.0, 4.0)
    return noise * envelope / jnp.sqrt(energy)[None, :]


def block_levels(rng, shape, shards, low, largest):
    level, own = 1.0, jax.random.fold_in(rng, 6)
    for position, shards_of in shards:
        heights = jnp.exp(jax.random.uniform(jax.random.fold_in(own, position), (shards_of,), jnp.float32, low / len(shards), largest / len(shards)))
        level = level * jnp.repeat(heights, shape[position] // shards_of).reshape([-1 if axis == position else 1 for axis in range(len(shape))])
    return level


def bell_draw(rng, extent, scale, reach, pieces=(), kind=jnp.bfloat16):
    array = jax.random.normal(rng, extent, jnp.float32) * scale
    if len(pieces) > 0:
        array = block_levels(rng, extent, pieces, -0.22, 0.18) * array
    return jnp.clip(array, min=-reach, max=reach).astype(kind)


def setup_inputs(seed: int = 0) -> dict:
    seeds = jax.random.split(jax.random.key(seed), 5)
    signal = bell_draw(seeds[0], (SEQS, LENGTH, CH), 1.0, 6.0, ((0, 32), (1, 16)))
    out_grad = bell_draw(seeds[1], (SEQS, LENGTH, CH), 1.0, 6.0, ((0, 32), (1, 16)))
    filt = draw_filt(jax.random.fold_in(seeds[4], 71), 0)
    skip = jnp.clip(jax.random.uniform(seeds[3], (CH,), jnp.float32, 0.5, 1.5), 0.5, 1.5)
    return dict(signal=signal, out_grad=out_grad, filt=filt, skip=skip)


def reference(signal, out_grad, filt, skip):
    length = signal.shape[1]
    period = 2 * length
    spec_h = jnp.fft.rfft(filt, n=period, axis=0)

    def one_sequence(running, seq_pair):
        signal_row = seq_pair[0].astype(jnp.float32)
        grad_row = seq_pair[1].astype(jnp.float32)
        spec_u = jnp.fft.rfft(signal_row, n=period, axis=0)
        spec_g = jnp.fft.rfft(grad_row, n=period, axis=0)
        back = jnp.fft.irfft(jnp.conj(spec_h) * spec_g, n=period, axis=0)[:length]
        grad_in = (back + skip[None, :] * grad_row).astype(jnp.bfloat16)
        return (running + spec_g * jnp.conj(spec_u), grad_in)
    start = jnp.zeros(spec_h.shape, spec_h.dtype)
    running, in_grad = lax.scan(one_sequence, start, (signal, out_grad))
    factor = 1.0 / math.sqrt(SEQS * LENGTH)
    filt_grad = jnp.fft.irfft(running, n=period, axis=0)[:length] * factor
    return (in_grad, filt_grad.astype(jnp.float32))
```

```python
import functools
import math

import jax
import jax.numpy as jnp
import ml_dtypes
import numpy as np
from jax import lax
from jax.experimental import pallas as pl
from jax.experimental.pallas import tpu as pltpu
from jax.sharding import PartitionSpec as P

SEQ, ZED, CORES = 16, 16, 2
PANEL, HALF, CH, OWN = 256, 128, 128, 8
FREQ = PANEL
F32, BF16 = jnp.float32, jnp.bfloat16
NT = (((1,), (1,)), ((), ()))
NN = (((1,), (0,)), ((), ()))


def table():
    product = np.arange(PANEL)[:, None] * (2 * np.arange(FREQ)[None, :] + 1) % (4 * PANEL)
    phase = 2.0 * math.pi / (4 * PANEL) * product.astype(np.float64)
    full = np.concatenate([np.cos(phase), -np.sin(phase)], axis=1)
    high = full.astype(ml_dtypes.bfloat16)
    rest = (full - high.astype(np.float64)).astype(ml_dtypes.bfloat16)
    return np.stack([high, rest])


def dot(a, b, dims):
    return lax.dot_general(a, b, dims, preferred_element_type=F32)


def split(x):
    high = x.astype(BF16)
    return high, (x - high.astype(F32)).astype(BF16)


def correlate(x_of, g_ref, v_ref):
    for lane in range(0, FREQ, HALF):
        total_re = total_im = None
        for a in range(SEQ):
            x_re, x_im = x_of(a, lane)
            g_re = g_ref[a:, :, lane : lane + HALF]
            g_im = g_ref[a:, :, FREQ + lane : FREQ + lane + HALF]
            new_re = x_re * g_re + x_im * g_im
            new_im = x_re * g_im - x_im * g_re
            if a == 0:
                total_re, total_im = new_re, new_im
            else:
                n = SEQ - a
                total_re = jnp.concatenate([total_re[:n] + new_re, total_re[n:]], axis=0)
                total_im = jnp.concatenate([total_im[:n] + new_im, total_im[n:]], axis=0)
        for total, first in ((total_re, lane), (total_im, FREQ + lane)):
            high, rest = split(total.reshape(SEQ * OWN, HALF))
            v_ref[0 : SEQ * OWN, first : first + HALF] = high
            v_ref[SEQ * OWN :, first : first + HALF] = rest


def kernel(
    u_ref, g_ref, f_ref, skip_ref, w_ref, in_ref, fg_ref,
    send_ug, recv_ug, send_f, recv_f, spec, spec_f, spin, v_ref, part, from_core, pair_sum, recv_z,
    own_sum, recv_s, send_in, recv_in, send_sem, recv_sem,
):
    me, dp = lax.axis_index("seq"), lax.axis_index("dp")
    z, core = lax.div(dp, CORES), lax.rem(dp, CORES)
    seq_peer = lambda k: lax.rem(me + k, SEQ)
    z_peer = lambda k: lax.rem(z + k, ZED)
    other = 1 - core

    barrier = pltpu.get_barrier_semaphore()
    for k in range(1, SEQ):
        pl.semaphore_signal(barrier, inc=1, device_id={"seq": seq_peer(k)})
    for k in range(1, ZED):
        pl.semaphore_signal(barrier, inc=1, device_id={"dp": z_peer(k) * CORES + core})
    pl.semaphore_signal(barrier, inc=1, device_id={"dp": z * CORES + other})

    def send(src, dst, place, device):
        pltpu.make_async_remote_copy(
            src_ref=src, dst_ref=dst, send_sem=send_sem.at[place], recv_sem=recv_sem.at[place], device_id=device
        ).start()

    def await_bytes(ref, sem, place):
        pltpu.make_async_copy(ref, ref, sem.at[place]).wait()

    rows = lax.broadcasted_iota(jnp.int32, (CH, CH), 0)
    eye = (rows == lax.broadcasted_iota(jnp.int32, (CH, CH), 1)).astype(F32).astype(BF16)

    def stage(first, second, out_ref):
        first, second = dot(eye, first, NT), dot(eye, second, NT)
        for h in range(2):
            lanes = slice(h * HALF, (h + 1) * HALF)
            tile = jnp.concatenate(
                [first[:, lanes].reshape(SEQ, OWN, HALF), second[:, lanes].reshape(SEQ, OWN, HALF)], axis=1
            )
            out_ref[:, h] = tile.astype(BF16)

    stage(u_ref[0], g_ref[0], send_ug)
    tap = lax.broadcasted_iota(jnp.int32, (PANEL, CH), 0) + me
    filt = f_ref[...] + jnp.where(tap == 0, jnp.broadcast_to(skip_ref[...], (PANEL, CH)), 0.0)
    stage(*split(filt), send_f)

    pl.semaphore_wait(barrier, SEQ + ZED - 1)
    for k in range(1, SEQ):
        peer = seq_peer(k)
        send(send_ug.at[peer], recv_ug.at[me], 0, {"seq": peer})
    for k in range(1, SEQ):
        peer = seq_peer(k)
        send(send_f.at[peer], recv_f.at[me], 1, {"seq": peer})
    recv_ug[me] = send_ug[me]
    recv_f[me] = send_f[me]

    def transform(tiles_ref):
        lhs = jnp.concatenate(
            [tiles_ref[:, 0].reshape(2 * SEQ * OWN, HALF), tiles_ref[:, 1].reshape(2 * SEQ * OWN, HALF)], axis=1
        )
        return dot(lhs, w_ref[0], NN) + dot(lhs, w_ref[1], NN)

    await_bytes(recv_ug.at[pl.ds(0, SEQ - 1)], recv_sem, 0)
    spec[...] = transform(recv_ug).reshape(SEQ, 2, OWN, 2 * FREQ)

    lanes = lax.broadcasted_iota(jnp.int32, (OWN, FREQ), 1)
    sign = 1.0 - 2.0 * lax.rem(lanes, 2).astype(F32)
    for a in range(SEQ):
        re, im = spec[a, 1, :, :FREQ], spec[a, 1, :, FREQ:]
        if a < SEQ - 1:
            re, im = re + sign * spec[a + 1, 1, :, FREQ:], im - sign * spec[a + 1, 1, :, :FREQ]
        spin[a, :, :FREQ] = re
        spin[a, :, FREQ:] = im

    correlate(
        lambda a, lane: (
            spec[a, 0, :, lane : lane + HALF], spec[a, 0, :, FREQ + lane : FREQ + lane + HALF]
        ),
        spin, v_ref,
    )
    wide = dot(w_ref[0], v_ref[...], NT)
    weight = wide[:, :CH] + wide[:, CH:] + dot(w_ref[1], v_ref[0 : SEQ * OWN], NT)
    weight = weight * (1.0 / (PANEL * math.sqrt(CORES * ZED * SEQ * PANEL)))
    weight = weight.reshape(ZED, CORES, OWN, CH)
    for side in range(CORES):
        part[side] = weight[:, side]
    send(part.at[other], from_core, 2, {"dp": z * CORES + other})

    await_bytes(recv_f.at[pl.ds(0, SEQ - 1)], recv_sem, 1)
    both = transform(recv_f).reshape(SEQ, 2, OWN, 2 * FREQ)
    spec_f[...] = both[:, 0] + both[:, 1]

    await_bytes(from_core, recv_sem, 2)
    pair_sum[...] = part[core] + from_core[...]
    for k in range(1, ZED):
        peer = z_peer(k)
        send(pair_sum.at[peer], recv_z.at[z], 3, {"dp": peer * CORES + core})
    recv_z[z] = pair_sum[z]

    correlate(
        lambda a, lane: (spec_f[a, :, lane : lane + HALF], spec_f[a, :, FREQ + lane : FREQ + lane + HALF]),
        spin, v_ref,
    )
    tall = dot(v_ref[...], w_ref[0], NT)
    back = tall[: SEQ * OWN] + tall[SEQ * OWN :] + dot(v_ref[0 : SEQ * OWN], w_ref[1], NT)
    back = (back * (1.0 / PANEL)).reshape(SEQ, OWN, PANEL)
    send_in[...] = jnp.concatenate([back[:, :, :HALF], back[:, :, HALF:]], axis=1).astype(BF16)
    for k in range(1, SEQ):
        peer = seq_peer(k)
        send(send_in.at[peer], recv_in.at[me], 4, {"seq": peer})
    recv_in[me] = send_in[me]

    await_bytes(recv_z.at[pl.ds(0, ZED - 1)], recv_sem, 3)
    own_sum[...] = jnp.sum(recv_z[...], axis=0)
    for k in range(1, SEQ):
        send(own_sum, recv_s.at[me], 5, {"seq": seq_peer(k)})
    recv_s[me] = own_sum[...]

    await_bytes(recv_in.at[pl.ds(0, SEQ - 1)], recv_sem, 4)
    for h in range(2):
        block = recv_in[...].astype(F32)[:, h * OWN : (h + 1) * OWN].reshape(CH, HALF)
        in_ref[0, h * HALF : (h + 1) * HALF] = block.T.astype(BF16)

    await_bytes(recv_s.at[pl.ds(0, SEQ - 1)], recv_sem, 5)
    group = lax.div(lax.broadcasted_iota(jnp.int32, (OWN, CH), 1), OWN)
    result = jnp.zeros((OWN, CH), F32)
    for s in range(SEQ):
        turned = pltpu.roll(recv_s[s], lax.rem(s + SEQ - me, SEQ) * OWN, 1)
        result = jnp.where(group == s, turned, result)
    fg_ref[...] = result

    await_bytes(send_ug.at[pl.ds(0, SEQ - 1)], send_sem, 0)
    await_bytes(send_f.at[pl.ds(0, SEQ - 1)], send_sem, 1)
    await_bytes(from_core, send_sem, 2)
    await_bytes(pair_sum.at[pl.ds(0, ZED - 1)], send_sem, 3)
    await_bytes(send_in.at[pl.ds(0, SEQ - 1)], send_sem, 4)
    await_bytes(recv_s.at[pl.ds(0, SEQ - 1)], send_sem, 5)


def on_device(signal, out_grad, filt, skip):
    vmem = pl.BlockSpec(memory_space=pltpu.VMEM)
    tiles = (SEQ, 2, 2 * OWN, HALF)
    return pl.pallas_call(
        kernel,
        out_shape=(
            jax.ShapeDtypeStruct((1, PANEL, CH), BF16),
            jax.ShapeDtypeStruct((OWN, CH), F32),
        ),
        in_specs=[vmem] * 5,
        out_specs=(vmem, vmem),
        scratch_shapes=[
            pltpu.VMEM(tiles, BF16),
            pltpu.VMEM(tiles, BF16),
            pltpu.VMEM(tiles, BF16),
            pltpu.VMEM(tiles, BF16),
            pltpu.VMEM((SEQ, 2, OWN, 2 * FREQ), F32),
            pltpu.VMEM((SEQ, OWN, 2 * FREQ), F32),
            pltpu.VMEM((SEQ, OWN, 2 * FREQ), F32),
            pltpu.VMEM((2 * SEQ * OWN, 2 * FREQ), BF16),
            pltpu.VMEM((CORES, ZED, OWN, CH), F32),
            pltpu.VMEM((ZED, OWN, CH), F32),
            pltpu.VMEM((ZED, OWN, CH), F32),
            pltpu.VMEM((ZED, OWN, CH), F32),
            pltpu.VMEM((OWN, CH), F32),
            pltpu.VMEM((SEQ, OWN, CH), F32),
            pltpu.VMEM((SEQ, 2 * OWN, HALF), BF16),
            pltpu.VMEM((SEQ, 2 * OWN, HALF), BF16),
            pltpu.SemaphoreType.DMA((6,)),
            pltpu.SemaphoreType.DMA((6,)),
        ],
        compiler_params=pltpu.CompilerParams(
            collective_id=0, has_side_effects=True, vmem_limit_bytes=32 * 1024 * 1024
        ),
    )(signal, out_grad, filt, skip.reshape(1, CH), jnp.asarray(table()))


def solution(mesh):
    placed = (P("dp", "seq", None), P("dp", "seq", None), P("seq", None), P())
    return jax.shard_map(
        on_device,
        mesh=mesh,
        in_specs=placed,
        out_specs=(P("dp", "seq", None), P(("seq", "dp"), None)),
        check_vma=False,
    )
```

```python
import functools
import math

import jax
import jax.numpy as jnp
import ml_dtypes
import numpy as np
from jax import lax
from jax.experimental import pallas as pl
from jax.experimental.pallas import tpu as pltpu
from jax.sharding import PartitionSpec as P

SEQ, ZED, CORES = 16, 16, 2
PANEL, HALF, CH, OWN = 256, 128, 128, 8
FREQ = PANEL
NEAR = 4
SEQ_OFFSETS = sorted(
    ((i, j) for i in range(4) for j in range(4) if i + j), key=lambda o: -sum(min(k, 4 - k) for k in o)
)
Z_OFFSETS = sorted(range(1, ZED), key=lambda k: -min(k, ZED - k))
F32, BF16 = jnp.float32, jnp.bfloat16
NT = (((1,), (1,)), ((), ()))
NN = (((1,), (0,)), ((), ()))


def table():
    product = np.arange(PANEL)[:, None] * (2 * np.arange(FREQ)[None, :] + 1) % (4 * PANEL)
    phase = 2.0 * math.pi / (4 * PANEL) * product.astype(np.float64)
    full = np.concatenate([np.cos(phase), -np.sin(phase)], axis=1)
    high = full.astype(ml_dtypes.bfloat16)
    rest = (full - high.astype(np.float64)).astype(ml_dtypes.bfloat16)
    return np.stack([high, rest])


def dot(a, b, dims):
    return lax.dot_general(a, b, dims, preferred_element_type=F32)


def split(x):
    high = x.astype(BF16)
    return high, (x - high.astype(F32)).astype(BF16)


def correlate(x_of, g_ref, v_ref):
    for lane in range(0, FREQ, HALF):
        total_re = total_im = None
        for a in range(SEQ):
            x_re, x_im = x_of(a, lane)
            g_re = g_ref[a:, :, lane : lane + HALF]
            g_im = g_ref[a:, :, FREQ + lane : FREQ + lane + HALF]
            new_re = x_re * g_re + x_im * g_im
            new_im = x_re * g_im - x_im * g_re
            if a == 0:
                total_re, total_im = new_re, new_im
            else:
                n = SEQ - a
                total_re = jnp.concatenate([total_re[:n] + new_re, total_re[n:]], axis=0)
                total_im = jnp.concatenate([total_im[:n] + new_im, total_im[n:]], axis=0)
        for total, first in ((total_re, lane), (total_im, FREQ + lane)):
            high, rest = split(total.reshape(SEQ * OWN, HALF))
            v_ref[0 : SEQ * OWN, first : first + HALF] = high
            v_ref[SEQ * OWN :, first : first + HALF] = rest


def kernel(
    u_hbm, g_hbm, f_hbm, skip_hbm, w_hbm, in_ref, fg_ref,
    u_ref, g_ref, f_ref, skip_ref, w_ref, send_ug, recv_ug, send_f, recv_f, spec, spec_f, spin, v_ref, part, from_core, pair_sum, recv_z,
    own_sum, recv_s, send_in, recv_in, send_sem, recv_sem, load_sem, relay_sem,
):
    me, dp = lax.axis_index("seq"), lax.axis_index("dp")
    z, core = lax.div(dp, CORES), lax.rem(dp, CORES)
    x, y = lax.div(me, 4), lax.rem(me, 4)
    seq_peers = [lax.rem(x + i, 4) * 4 + lax.rem(y + j, 4) for i, j in SEQ_OFFSETS]
    z_peer = lambda k: lax.rem(z + k, ZED)
    other = 1 - core

    loads = [
        pltpu.make_async_copy(src, dst, load_sem.at[i])
        for i, (src, dst) in enumerate(
            ((u_hbm, u_ref), (g_hbm, g_ref), (f_hbm, f_ref), (skip_hbm, skip_ref), (w_hbm, w_ref))
        )
    ]
    for load in loads[:2]:
        load.start()
    barrier = pltpu.get_barrier_semaphore()
    for k in Z_OFFSETS[-2 * NEAR :]:
        pl.semaphore_signal(barrier, inc=1, device_id={"dp": z_peer(k) * CORES + core})
    for peer in seq_peers:
        pl.semaphore_signal(barrier, inc=1, device_id={"seq": peer})
    pl.semaphore_signal(barrier, inc=1, device_id={"dp": z * CORES + other})

    for load in loads[2:]:
        load.start()

    def send(src, dst, place, device):
        pltpu.make_async_remote_copy(
            src_ref=src, dst_ref=dst, send_sem=send_sem.at[place], recv_sem=recv_sem.at[place], device_id=device
        ).start()

    def await_bytes(ref, sem, place):
        pltpu.make_async_copy(ref, ref, sem.at[place]).wait()

    rows = lax.broadcasted_iota(jnp.int32, (CH, CH), 0)
    eye = (rows == lax.broadcasted_iota(jnp.int32, (CH, CH), 1)).astype(F32).astype(BF16)

    def stage(first, second, out_ref):
        first, second = dot(eye, first, NT), dot(eye, second, NT)
        for h in range(2):
            lanes = slice(h * HALF, (h + 1) * HALF)
            tile = jnp.concatenate(
                [first[:, lanes].reshape(SEQ, OWN, HALF), second[:, lanes].reshape(SEQ, OWN, HALF)], axis=1
            )
            out_ref[:, h] = tile.astype(BF16)

    loads[0].wait()
    loads[1].wait()
    stage(u_ref[0], g_ref[0], send_ug)
    loads[2].wait()
    loads[3].wait()
    tap = lax.broadcasted_iota(jnp.int32, (PANEL, CH), 0) + me
    filt = f_ref[...] + jnp.where(tap == 0, jnp.broadcast_to(skip_ref[...], (PANEL, CH)), 0.0)
    stage(*split(filt), send_f)

    pl.semaphore_wait(barrier, SEQ + 2 * NEAR)
    for k in (NEAR, ZED - NEAR):
        pl.semaphore_signal(relay_sem, inc=1, device_id={"dp": z_peer(k) * CORES + core})
    for peer in seq_peers:
        send(send_ug.at[peer], recv_ug.at[me], 0, {"seq": peer})
    for peer in seq_peers:
        send(send_f.at[peer], recv_f.at[me], 1, {"seq": peer})
    recv_ug[me] = send_ug[me]
    recv_f[me] = send_f[me]

    loads[4].wait()

    def transform(tiles_ref):
        lhs = jnp.concatenate(
            [tiles_ref[:, 0].reshape(2 * SEQ * OWN, HALF), tiles_ref[:, 1].reshape(2 * SEQ * OWN, HALF)], axis=1
        )
        return dot(lhs, w_ref[0], NN) + dot(lhs, w_ref[1], NN)

    await_bytes(recv_ug.at[pl.ds(0, SEQ - 1)], recv_sem, 0)
    spec[...] = transform(recv_ug).reshape(SEQ, 2, OWN, 2 * FREQ)

    lanes = lax.broadcasted_iota(jnp.int32, (OWN, FREQ), 1)
    sign = 1.0 - 2.0 * lax.rem(lanes, 2).astype(F32)
    for a in range(SEQ):
        re, im = spec[a, 1, :, :FREQ], spec[a, 1, :, FREQ:]
        if a < SEQ - 1:
            re, im = re + sign * spec[a + 1, 1, :, FREQ:], im - sign * spec[a + 1, 1, :, :FREQ]
        spin[a, :, :FREQ] = re
        spin[a, :, FREQ:] = im

    correlate(
        lambda a, lane: (
            spec[a, 0, :, lane : lane + HALF], spec[a, 0, :, FREQ + lane : FREQ + lane + HALF]
        ),
        spin, v_ref,
    )
    wide = dot(w_ref[0], v_ref[...], NT)
    weight = wide[:, :CH] + wide[:, CH:] + dot(w_ref[1], v_ref[0 : SEQ * OWN], NT)
    weight = weight * (1.0 / (PANEL * math.sqrt(CORES * ZED * SEQ * PANEL)))
    weight = weight.reshape(ZED, CORES, OWN, CH)
    for side in range(CORES):
        part[side] = weight[:, side]
    send(part.at[other], from_core, 2, {"dp": z * CORES + other})

    await_bytes(recv_f.at[pl.ds(0, SEQ - 1)], recv_sem, 1)
    both = transform(recv_f).reshape(SEQ, 2, OWN, 2 * FREQ)
    spec_f[...] = both[:, 0] + both[:, 1]

    await_bytes(from_core, recv_sem, 2)
    pair_sum[...] = part[core] + from_core[...]
    pl.semaphore_wait(relay_sem, 2)
    for k in Z_OFFSETS:
        peer = z_peer(k)
        send(pair_sum.at[peer], recv_z.at[z], 3, {"dp": peer * CORES + core})
    recv_z[z] = pair_sum[z]

    correlate(
        lambda a, lane: (spec_f[a, :, lane : lane + HALF], spec_f[a, :, FREQ + lane : FREQ + lane + HALF]),
        spin, v_ref,
    )
    tall = dot(v_ref[...], w_ref[0], NT)
    back = tall[: SEQ * OWN] + tall[SEQ * OWN :] + dot(v_ref[0 : SEQ * OWN], w_ref[1], NT)
    back = (back * (1.0 / PANEL)).reshape(SEQ, OWN, PANEL)
    send_in[...] = jnp.concatenate([back[:, :, :HALF], back[:, :, HALF:]], axis=1).astype(BF16)
    for peer in seq_peers:
        send(send_in.at[peer], recv_in.at[me], 4, {"seq": peer})
    recv_in[me] = send_in[me]

    await_bytes(recv_z.at[pl.ds(0, ZED - 1)], recv_sem, 3)
    own_sum[...] = jnp.sum(recv_z[...], axis=0)
    for peer in seq_peers:
        send(own_sum, recv_s.at[me], 5, {"seq": peer})
    recv_s[me] = own_sum[...]

    await_bytes(recv_in.at[pl.ds(0, SEQ - 1)], recv_sem, 4)
    for h in range(2):
        block = recv_in[...].astype(F32)[:, h * OWN : (h + 1) * OWN].reshape(CH, HALF)
        in_ref[0, h * HALF : (h + 1) * HALF] = block.T.astype(BF16)

    await_bytes(recv_s.at[pl.ds(0, SEQ - 1)], recv_sem, 5)
    group = lax.div(lax.broadcasted_iota(jnp.int32, (OWN, CH), 1), OWN)
    result = jnp.zeros((OWN, CH), F32)
    for s in range(SEQ):
        turned = pltpu.roll(recv_s[s], lax.rem(s + SEQ - me, SEQ) * OWN, 1)
        result = jnp.where(group == s, turned, result)
    fg_ref[...] = result

    await_bytes(send_ug.at[pl.ds(0, SEQ - 1)], send_sem, 0)
    await_bytes(send_f.at[pl.ds(0, SEQ - 1)], send_sem, 1)
    await_bytes(from_core, send_sem, 2)
    await_bytes(pair_sum.at[pl.ds(0, ZED - 1)], send_sem, 3)
    await_bytes(send_in.at[pl.ds(0, SEQ - 1)], send_sem, 4)
    await_bytes(recv_s.at[pl.ds(0, SEQ - 1)], send_sem, 5)


def on_device(signal, out_grad, filt, skip):
    vmem = pl.BlockSpec(memory_space=pltpu.VMEM)
    operands = (signal, out_grad, filt, skip.reshape(1, CH), jnp.asarray(table()))
    tiles = (SEQ, 2, 2 * OWN, HALF)
    return pl.pallas_call(
        kernel,
        out_shape=(
            pltpu.VMEM((1, PANEL, CH), BF16),
            pltpu.VMEM((OWN, CH), F32),
        ),
        in_specs=[pl.BlockSpec(memory_space=pltpu.HBM)] * 5,
        out_specs=(vmem, vmem),
        scratch_shapes=[
            pltpu.VMEM((1, PANEL, CH), BF16),
            pltpu.VMEM((1, PANEL, CH), BF16),
            pltpu.VMEM((PANEL, CH), F32),
            pltpu.VMEM((1, CH), F32),
            pltpu.VMEM((2, PANEL, 2 * FREQ), BF16),
            pltpu.VMEM(tiles, BF16),
            pltpu.VMEM(tiles, BF16),
            pltpu.VMEM(tiles, BF16),
            pltpu.VMEM(tiles, BF16),
            pltpu.VMEM((SEQ, 2, OWN, 2 * FREQ), F32),
            pltpu.VMEM((SEQ, OWN, 2 * FREQ), F32),
            pltpu.VMEM((SEQ, OWN, 2 * FREQ), F32),
            pltpu.VMEM((2 * SEQ * OWN, 2 * FREQ), BF16),
            pltpu.VMEM((CORES, ZED, OWN, CH), F32),
            pltpu.VMEM((ZED, OWN, CH), F32),
            pltpu.VMEM((ZED, OWN, CH), F32),
            pltpu.VMEM((ZED, OWN, CH), F32),
            pltpu.VMEM((OWN, CH), F32),
            pltpu.VMEM((SEQ, OWN, CH), F32),
            pltpu.VMEM((SEQ, 2 * OWN, HALF), BF16),
            pltpu.VMEM((SEQ, 2 * OWN, HALF), BF16),
            pltpu.SemaphoreType.DMA((6,)),
            pltpu.SemaphoreType.DMA((6,)),
            pltpu.SemaphoreType.DMA((5,)),
            pltpu.SemaphoreType.REGULAR,
        ],
        compiler_params=pltpu.CompilerParams(
            collective_id=0, has_side_effects=True, vmem_limit_bytes=16 * 1024 * 1024
        ),
    )(*(pltpu.with_memory_space_constraint(x, pltpu.HBM) for x in operands))


def solution(mesh):
    placed = (P("dp", "seq", None), P("dp", "seq", None), P("seq", None), P())
    return jax.shard_map(
        on_device,
        mesh=mesh,
        in_specs=placed,
        out_specs=(P("dp", "seq", None), P(("seq", "dp"), None)),
        check_vma=False,
    )
```

```python
import functools
import math

import jax
import jax.numpy as jnp
import ml_dtypes
import numpy as np
from jax import lax
from jax.experimental import pallas as pl
from jax.experimental.pallas import tpu as pltpu
from jax.sharding import PartitionSpec as P

SEQ, ZED, CORES = 16, 16, 2
PANEL, HALF, CH, OWN = 256, 128, 128, 8
FREQ = PANEL
NEAR = 4
EARLY = (1,)
SEQ_OFFSETS = sorted(
    ((i, j) for i in range(4) for j in range(4) if i + j), key=lambda o: -sum(min(k, 4 - k) for k in o)
)
Z_OFFSETS = sorted(range(1, ZED), key=lambda k: -min(k, ZED - k))
F32, BF16 = jnp.float32, jnp.bfloat16
NT = (((1,), (1,)), ((), ()))
NN = (((1,), (0,)), ((), ()))


def table():
    product = np.arange(PANEL)[:, None] * (2 * np.arange(FREQ)[None, :] + 1) % (4 * PANEL)
    phase = 2.0 * math.pi / (4 * PANEL) * product.astype(np.float64)
    full = np.concatenate([np.cos(phase), -np.sin(phase)], axis=1)
    high = full.astype(ml_dtypes.bfloat16)
    rest = (full - high.astype(np.float64)).astype(ml_dtypes.bfloat16)
    return np.stack([high, rest])


def dot(a, b, dims):
    return lax.dot_general(a, b, dims, preferred_element_type=F32)


def split(x):
    high = x.astype(BF16)
    return high, (x - high.astype(F32)).astype(BF16)


def correlate(x_of, g_ref, v_ref):
    for lane in range(0, FREQ, HALF):
        total_re = total_im = None
        for a in range(SEQ):
            x_re, x_im = x_of(a, lane)
            g_re = g_ref[a:, :, lane : lane + HALF]
            g_im = g_ref[a:, :, FREQ + lane : FREQ + lane + HALF]
            new_re = x_re * g_re + x_im * g_im
            new_im = x_re * g_im - x_im * g_re
            if a == 0:
                total_re, total_im = new_re, new_im
            else:
                n = SEQ - a
                total_re = jnp.concatenate([total_re[:n] + new_re, total_re[n:]], axis=0)
                total_im = jnp.concatenate([total_im[:n] + new_im, total_im[n:]], axis=0)
        for total, first in ((total_re, lane), (total_im, FREQ + lane)):
            high, rest = split(total.reshape(SEQ * OWN, HALF))
            v_ref[0 : SEQ * OWN, first : first + HALF] = high
            v_ref[SEQ * OWN :, first : first + HALF] = rest


def beside(dp, place):
    near = min((dp // CORES - place // CORES) % ZED, (place // CORES - dp // CORES) % ZED)
    return near == 0 or (near <= NEAR and dp % CORES == place % CORES)


def kernel(
    u_hbm, g_hbm, f_hbm, skip_hbm, w_hbm, in_ref, fg_ref,
    u_ref, g_ref, f_ref, skip_ref, w_ref, send_ug, recv_ug, send_f, recv_f, spec, spec_f, spin, v_ref, part, from_core, pair_sum, recv_z,
    own_sum, recv_s, send_in, recv_in, send_sem, recv_sem, load_sem, relay_sem, vouch_sem, early_row, recv_early,
):
    me, dp = lax.axis_index("seq"), lax.axis_index("dp")
    z, core = lax.div(dp, CORES), lax.rem(dp, CORES)
    x, y = lax.div(me, 4), lax.rem(me, 4)
    seq_peers = [lax.rem(x + i, 4) * 4 + lax.rem(y + j, 4) for i, j in SEQ_OFFSETS]
    z_peer = lambda k: lax.rem(z + k, ZED)
    other = 1 - core

    loads = [
        pltpu.make_async_copy(src, dst, load_sem.at[i])
        for i, (src, dst) in enumerate(
            ((u_hbm, u_ref), (g_hbm, g_ref), (f_hbm, f_ref), (skip_hbm, skip_ref), (w_hbm, w_ref))
        )
    ]
    for load in loads[:2]:
        load.start()
    barrier = pltpu.get_barrier_semaphore()
    for k in Z_OFFSETS[-2 * NEAR :]:
        pl.semaphore_signal(barrier, inc=1, device_id={"dp": z_peer(k) * CORES + core})
    for peer in seq_peers:
        pl.semaphore_signal(barrier, inc=1, device_id={"seq": peer})
    pl.semaphore_signal(barrier, inc=1, device_id={"dp": z * CORES + other})

    for load in loads[2:]:
        load.start()

    early_dp = (dp >= EARLY[0]) & (dp <= EARLY[-1])
    early = (me == 0) & early_dp

    greetings = SEQ + 2 * NEAR
    for place in EARLY:
        strangers = [k for k in range(CORES * ZED) if not beside(k, place)]
        unknown = functools.reduce(jnp.logical_or, [dp == k for k in strangers])
        greetings += jnp.where((me == 0) & unknown, 1, 0)

        @pl.when((me == 0) & (dp == place))
        def _():
            for k in strangers:
                pl.semaphore_signal(barrier, inc=1, device_id={"dp": k})

    def send(src, dst, place, device):
        pltpu.make_async_remote_copy(
            src_ref=src, dst_ref=dst, send_sem=send_sem.at[place], recv_sem=recv_sem.at[place], device_id=device
        ).start()

    def await_bytes(ref, sem, place):
        pltpu.make_async_copy(ref, ref, sem.at[place]).wait()

    rows = lax.broadcasted_iota(jnp.int32, (CH, CH), 0)
    eye = (rows == lax.broadcasted_iota(jnp.int32, (CH, CH), 1)).astype(F32).astype(BF16)

    def stage(first, second, out_ref):
        first, second = dot(eye, first, NT), dot(eye, second, NT)
        for h in range(2):
            lanes = slice(h * HALF, (h + 1) * HALF)
            tile = jnp.concatenate(
                [first[:, lanes].reshape(SEQ, OWN, HALF), second[:, lanes].reshape(SEQ, OWN, HALF)], axis=1
            )
            out_ref[:, h] = tile.astype(BF16)

    loads[0].wait()
    loads[1].wait()
    stage(u_ref[0], g_ref[0], send_ug)
    loads[2].wait()
    loads[3].wait()
    tap = lax.broadcasted_iota(jnp.int32, (PANEL, CH), 0) + me
    filt = f_ref[...] + jnp.where(tap == 0, jnp.broadcast_to(skip_ref[...], (PANEL, CH)), 0.0)
    stage(*split(filt), send_f)

    pl.semaphore_wait(barrier, greetings)
    for k in (NEAR, ZED - NEAR):
        pl.semaphore_signal(relay_sem, inc=1, device_id={"dp": z_peer(k) * CORES + core})

    @pl.when(me == 0)
    def _():
        for peer in seq_peers:
            pl.semaphore_signal(vouch_sem, inc=1, device_id={"seq": peer})

    for peer in seq_peers:
        send(send_ug.at[peer], recv_ug.at[me], 0, {"seq": peer})
    for peer in seq_peers:
        send(send_f.at[peer], recv_f.at[me], 1, {"seq": peer})
    recv_ug[me] = send_ug[me]
    recv_f[me] = send_f[me]

    loads[4].wait()

    def transform(tiles_ref):
        lhs = jnp.concatenate(
            [tiles_ref[:, 0].reshape(2 * SEQ * OWN, HALF), tiles_ref[:, 1].reshape(2 * SEQ * OWN, HALF)], axis=1
        )
        return dot(lhs, w_ref[0], NN) + dot(lhs, w_ref[1], NN)

    await_bytes(recv_ug.at[pl.ds(0, SEQ - 1)], recv_sem, 0)
    spec[...] = transform(recv_ug).reshape(SEQ, 2, OWN, 2 * FREQ)

    lanes = lax.broadcasted_iota(jnp.int32, (OWN, FREQ), 1)
    sign = 1.0 - 2.0 * lax.rem(lanes, 2).astype(F32)
    for a in range(SEQ):
        re, im = spec[a, 1, :, :FREQ], spec[a, 1, :, FREQ:]
        if a < SEQ - 1:
            re, im = re + sign * spec[a + 1, 1, :, FREQ:], im - sign * spec[a + 1, 1, :, :FREQ]
        spin[a, :, :FREQ] = re
        spin[a, :, FREQ:] = im

    correlate(
        lambda a, lane: (
            spec[a, 0, :, lane : lane + HALF], spec[a, 0, :, FREQ + lane : FREQ + lane + HALF]
        ),
        spin, v_ref,
    )
    wide = dot(w_ref[0], v_ref[...], NT)
    weight = wide[:, :CH] + wide[:, CH:] + dot(w_ref[1], v_ref[0 : SEQ * OWN], NT)
    weight = weight * (1.0 / (PANEL * math.sqrt(CORES * ZED * SEQ * PANEL)))
    group = lax.div(lax.broadcasted_iota(jnp.int32, (2 * OWN, CH), 1), OWN)
    line = lax.broadcasted_iota(jnp.int32, (2 * OWN, CH), 0)

    @pl.when(me > 0)
    def _():
        pl.semaphore_wait(vouch_sem, 1)

    for i, place in enumerate(EARLY):
        turned = pltpu.roll(weight[place * OWN : (place + 1) * OWN], 0, 1, stride=OWN, stride_axis=0)
        row = jnp.sum(jnp.where(group[:OWN] == line[:OWN], turned, 0.0), axis=0, keepdims=True)
        early_row[i : i + 1] = row
        here = early & (dp == place)

        @pl.when(here)
        def _():
            recv_early[pl.ds(dp * SEQ + me, 1)] = row

        @pl.when(jnp.logical_not(here))
        def _():
            send(
                early_row.at[pl.ds(i, 1)], recv_early.at[pl.ds(dp * SEQ + me, 1)], 6,
                {"seq": 0, "dp": place},
            )

    weight = weight.reshape(ZED, CORES, OWN, CH)
    for side in range(CORES):
        part[side] = weight[:, side]
    send(part.at[other], from_core, 2, {"dp": z * CORES + other})

    await_bytes(recv_f.at[pl.ds(0, SEQ - 1)], recv_sem, 1)
    both = transform(recv_f).reshape(SEQ, 2, OWN, 2 * FREQ)
    spec_f[...] = both[:, 0] + both[:, 1]

    await_bytes(from_core, recv_sem, 2)
    pair_sum[...] = part[core] + from_core[...]
    pl.semaphore_wait(relay_sem, 2)
    for k in Z_OFFSETS:
        peer = z_peer(k)
        send(pair_sum.at[peer], recv_z.at[z], 3, {"dp": peer * CORES + core})
    recv_z[z] = pair_sum[z]

    correlate(
        lambda a, lane: (spec_f[a, :, lane : lane + HALF], spec_f[a, :, FREQ + lane : FREQ + lane + HALF]),
        spin, v_ref,
    )
    tall = dot(v_ref[...], w_ref[0], NT)
    back = tall[: SEQ * OWN] + tall[SEQ * OWN :] + dot(v_ref[0 : SEQ * OWN], w_ref[1], NT)
    back = (back * (1.0 / PANEL)).reshape(SEQ, OWN, PANEL)
    send_in[...] = jnp.concatenate([back[:, :, :HALF], back[:, :, HALF:]], axis=1).astype(BF16)
    for peer in seq_peers:
        send(send_in.at[peer], recv_in.at[me], 4, {"seq": peer})
    recv_in[me] = send_in[me]

    await_bytes(recv_z.at[pl.ds(0, ZED - 1)], recv_sem, 3)
    own_sum[...] = jnp.sum(recv_z[...], axis=0)
    for peer in seq_peers:
        @pl.when(jnp.logical_not(early_dp & (peer == 0)))
        def _():
            send(own_sum, recv_s.at[me], 5, {"seq": peer})

    recv_s[me] = own_sum[...]

    await_bytes(recv_in.at[pl.ds(0, SEQ - 1)], recv_sem, 4)
    for h in range(2):
        block = recv_in[...].astype(F32)[:, h * OWN : (h + 1) * OWN].reshape(CH, HALF)
        in_ref[0, h * HALF : (h + 1) * HALF] = block.T.astype(BF16)

    @pl.when(jnp.logical_not(early))
    def _():
        await_bytes(recv_s.at[pl.ds(0, SEQ - 1)], recv_sem, 5)
        result = jnp.zeros((OWN, CH), F32)
        for s in range(SEQ):
            turned = pltpu.roll(recv_s[s], lax.rem(s + SEQ - me, SEQ) * OWN, 1)
            result = jnp.where(group[:OWN] == s, turned, result)
        fg_ref[...] = result

    @pl.when(early)
    def _():
        await_bytes(recv_early.at[pl.ds(0, SEQ * CORES * ZED - 1)], recv_sem, 6)
        total = jnp.sum(recv_early[...].reshape(CORES * ZED, SEQ, CH), axis=0)
        turned = pltpu.roll(total, 0, 1, stride=OWN, stride_axis=0)
        for r in range(OWN):
            shifted = turned if r == 0 else pltpu.roll(turned, CH - r * OWN, 1)
            fg_ref[r : r + 1] = jnp.sum(jnp.where(group == line, shifted, 0.0), axis=0, keepdims=True)

    await_bytes(send_ug.at[pl.ds(0, SEQ - 1)], send_sem, 0)
    await_bytes(send_f.at[pl.ds(0, SEQ - 1)], send_sem, 1)
    await_bytes(from_core, send_sem, 2)
    await_bytes(pair_sum.at[pl.ds(0, ZED - 1)], send_sem, 3)
    await_bytes(send_in.at[pl.ds(0, SEQ - 1)], send_sem, 4)
    sent = jnp.where(early_dp & (me > 0), SEQ - 2, SEQ - 1)

    def sent_one(i, carry):
        await_bytes(own_sum, send_sem, 5)
        return carry

    lax.fori_loop(0, sent, sent_one, 0)
    if len(EARLY) > 1:
        await_bytes(early_row.at[pl.ds(0, len(EARLY) - 1)], send_sem, 6)

    @pl.when(jnp.logical_not(early))
    def _():
        await_bytes(early_row.at[pl.ds(0, 1)], send_sem, 6)


def place(in_vmem, fg_vmem, in_hbm, fg_hbm, sem):
    copies = [
        pltpu.make_async_copy(in_vmem, in_hbm, sem.at[0]),
        pltpu.make_async_copy(fg_vmem, fg_hbm, sem.at[1]),
    ]
    for copy in copies:
        copy.start()
    for copy in copies:
        copy.wait()


def on_device(signal, out_grad, filt, skip):
    vmem = pl.BlockSpec(memory_space=pltpu.VMEM)
    operands = (signal, out_grad, filt, skip.reshape(1, CH), jnp.asarray(table()))
    tiles = (SEQ, 2, 2 * OWN, HALF)
    grads = pl.pallas_call(
        kernel,
        out_shape=(
            pltpu.VMEM((1, PANEL, CH), BF16),
            pltpu.VMEM((OWN, CH), F32),
        ),
        in_specs=[pl.BlockSpec(memory_space=pltpu.HBM)] * 5,
        out_specs=(vmem, vmem),
        scratch_shapes=[
            pltpu.VMEM((1, PANEL, CH), BF16),
            pltpu.VMEM((1, PANEL, CH), BF16),
            pltpu.VMEM((PANEL, CH), F32),
            pltpu.VMEM((1, CH), F32),
            pltpu.VMEM((2, PANEL, 2 * FREQ), BF16),
            pltpu.VMEM(tiles, BF16),
            pltpu.VMEM(tiles, BF16),
            pltpu.VMEM(tiles, BF16),
            pltpu.VMEM(tiles, BF16),
            pltpu.VMEM((SEQ, 2, OWN, 2 * FREQ), F32),
            pltpu.VMEM((SEQ, OWN, 2 * FREQ), F32),
            pltpu.VMEM((SEQ, OWN, 2 * FREQ), F32),
            pltpu.VMEM((2 * SEQ * OWN, 2 * FREQ), BF16),
            pltpu.VMEM((CORES, ZED, OWN, CH), F32),
            pltpu.VMEM((ZED, OWN, CH), F32),
            pltpu.VMEM((ZED, OWN, CH), F32),
            pltpu.VMEM((ZED, OWN, CH), F32),
            pltpu.VMEM((OWN, CH), F32),
            pltpu.VMEM((SEQ, OWN, CH), F32),
            pltpu.VMEM((SEQ, 2 * OWN, HALF), BF16),
            pltpu.VMEM((SEQ, 2 * OWN, HALF), BF16),
            pltpu.SemaphoreType.DMA((7,)),
            pltpu.SemaphoreType.DMA((7,)),
            pltpu.SemaphoreType.DMA((5,)),
            pltpu.SemaphoreType.REGULAR,
            pltpu.SemaphoreType.REGULAR,
            pltpu.VMEM((OWN, CH), F32),
            pltpu.VMEM((SEQ * CORES * ZED, CH), F32),
        ],
        compiler_params=pltpu.CompilerParams(
            collective_id=0, has_side_effects=True, vmem_limit_bytes=16 * 1024 * 1024
        ),
    )(*(pltpu.with_memory_space_constraint(x, pltpu.HBM) for x in operands))
    return pl.pallas_call(
        place,
        out_shape=(
            jax.ShapeDtypeStruct((1, PANEL, CH), BF16),
            jax.ShapeDtypeStruct((OWN, CH), F32),
        ),
        in_specs=[vmem] * 2,
        out_specs=(pl.BlockSpec(memory_space=pltpu.HBM),) * 2,
        scratch_shapes=[pltpu.SemaphoreType.DMA((2,))],
        compiler_params=pltpu.CompilerParams(vmem_limit_bytes=1024 * 1024),
    )(*grads)


def solution(mesh):
    placed = (P("dp", "seq", None), P("dp", "seq", None), P("seq", None), P())
    return jax.shard_map(
        on_device,
        mesh=mesh,
        in_specs=placed,
        out_specs=(P("dp", "seq", None), P(("seq", "dp"), None)),
        check_vma=False,
    )
```

```python
import functools
import math

import jax
import jax.numpy as jnp
import ml_dtypes
import numpy as np
from jax import lax
from jax.experimental import pallas as pl
from jax.experimental.pallas import tpu as pltpu
from jax.sharding import PartitionSpec as P

SEQ, ZED, CORES = 16, 16, 2
PANEL, HALF, CH, OWN = 256, 128, 128, 8
FREQ = PANEL
NEAR = 4
EARLY = (1,)
SEQ_OFFSETS = sorted(
    ((i, j) for i in range(4) for j in range(4) if i + j), key=lambda o: -sum(min(k, 4 - k) for k in o)
)
Z_OFFSETS = sorted(range(1, ZED), key=lambda k: -min(k, ZED - k))
FAR, NEARER = Z_OFFSETS[:3], Z_OFFSETS[3:]
F32, BF16 = jnp.float32, jnp.bfloat16
NT = (((1,), (1,)), ((), ()))
NN = (((1,), (0,)), ((), ()))


def table():
    product = np.arange(PANEL)[:, None] * (2 * np.arange(FREQ)[None, :] + 1) % (4 * PANEL)
    phase = 2.0 * math.pi / (4 * PANEL) * product.astype(np.float64)
    full = np.concatenate([np.cos(phase), -np.sin(phase)], axis=1)
    high = full.astype(ml_dtypes.bfloat16)
    rest = (full - high.astype(np.float64)).astype(ml_dtypes.bfloat16)
    return np.stack([high, rest])


def dot(a, b, dims):
    return lax.dot_general(a, b, dims, preferred_element_type=F32)


def split(x):
    high = x.astype(BF16)
    return high, (x - high.astype(F32)).astype(BF16)


def correlate(x_of, g_ref, v_ref):
    for lane in range(0, FREQ, HALF):
        total_re = total_im = None
        for a in range(SEQ):
            x_re, x_im = x_of(a, lane)
            g_re = g_ref[a:, :, lane : lane + HALF]
            g_im = g_ref[a:, :, FREQ + lane : FREQ + lane + HALF]
            new_re = x_re * g_re + x_im * g_im
            new_im = x_re * g_im - x_im * g_re
            if a == 0:
                total_re, total_im = new_re, new_im
            else:
                n = SEQ - a
                total_re = jnp.concatenate([total_re[:n] + new_re, total_re[n:]], axis=0)
                total_im = jnp.concatenate([total_im[:n] + new_im, total_im[n:]], axis=0)
        for total, first in ((total_re, lane), (total_im, FREQ + lane)):
            high, rest = split(total.reshape(SEQ * OWN, HALF))
            v_ref[0 : SEQ * OWN, first : first + HALF] = high
            v_ref[SEQ * OWN :, first : first + HALF] = rest


def beside(dp, place):
    near = min((dp // CORES - place // CORES) % ZED, (place // CORES - dp // CORES) % ZED)
    return near == 0 or (near <= NEAR and dp % CORES == place % CORES)


def kernel(
    u_hbm, g_hbm, f_hbm, skip_hbm, w_hbm, in_ref, fg_ref,
    u_ref, g_ref, f_ref, skip_ref, w_ref, send_ug, recv_ug, send_f, recv_f, spec, spec_f, spin, v_ref, part, from_core, pair_sum, recv_z,
    own_sum, recv_s, send_in, recv_in, send_sem, recv_sem, load_sem, relay_sem, vouch_sem, pair_sem, recv_far, early_row, recv_early,
):
    me, dp = lax.axis_index("seq"), lax.axis_index("dp")
    z, core = lax.div(dp, CORES), lax.rem(dp, CORES)
    x, y = lax.div(me, 4), lax.rem(me, 4)
    seq_peers = [lax.rem(x + i, 4) * 4 + lax.rem(y + j, 4) for i, j in SEQ_OFFSETS]
    z_peer = lambda k: lax.rem(z + k, ZED)
    other = 1 - core

    loads = [
        pltpu.make_async_copy(src, dst, load_sem.at[i])
        for i, (src, dst) in enumerate(
            ((u_hbm, u_ref), (g_hbm, g_ref), (f_hbm, f_ref), (skip_hbm, skip_ref), (w_hbm, w_ref))
        )
    ]
    for load in loads[:2]:
        load.start()
    barrier = pltpu.get_barrier_semaphore()
    for k in Z_OFFSETS[-2 * NEAR :]:
        pl.semaphore_signal(barrier, inc=1, device_id={"dp": z_peer(k) * CORES + core})
    for peer in seq_peers:
        pl.semaphore_signal(barrier, inc=1, device_id={"seq": peer})
    pl.semaphore_signal(barrier, inc=1, device_id={"dp": z * CORES + other})

    for load in loads[2:]:
        load.start()

    early_dp = (dp >= EARLY[0]) & (dp <= EARLY[-1])
    early = (me == 0) & early_dp

    greetings = SEQ + 2 * NEAR
    for place in EARLY:
        strangers = [k for k in range(CORES * ZED) if not beside(k, place)]
        unknown = functools.reduce(jnp.logical_or, [dp == k for k in strangers])
        greetings += jnp.where((me == 0) & unknown, 1, 0)

        @pl.when((me == 0) & (dp == place))
        def _():
            for k in strangers:
                pl.semaphore_signal(barrier, inc=1, device_id={"dp": k})

    def send(src, dst, place, device):
        pltpu.make_async_remote_copy(
            src_ref=src, dst_ref=dst, send_sem=send_sem.at[place], recv_sem=recv_sem.at[place], device_id=device
        ).start()

    def await_bytes(ref, sem, place):
        pltpu.make_async_copy(ref, ref, sem.at[place]).wait()

    rows = lax.broadcasted_iota(jnp.int32, (CH, CH), 0)
    eye = (rows == lax.broadcasted_iota(jnp.int32, (CH, CH), 1)).astype(F32).astype(BF16)

    def stage(first, second, out_ref):
        first, second = dot(eye, first, NT), dot(eye, second, NT)
        for h in range(2):
            lanes = slice(h * HALF, (h + 1) * HALF)
            tile = jnp.concatenate(
                [first[:, lanes].reshape(SEQ, OWN, HALF), second[:, lanes].reshape(SEQ, OWN, HALF)], axis=1
            )
            out_ref[:, h] = tile.astype(BF16)

    loads[0].wait()
    loads[1].wait()
    stage(u_ref[0], g_ref[0], send_ug)
    loads[2].wait()
    loads[3].wait()
    tap = lax.broadcasted_iota(jnp.int32, (PANEL, CH), 0) + me
    filt = f_ref[...] + jnp.where(tap == 0, jnp.broadcast_to(skip_ref[...], (PANEL, CH)), 0.0)
    stage(*split(filt), send_f)

    pl.semaphore_wait(barrier, greetings)
    for k in (NEAR, ZED - NEAR):
        pl.semaphore_signal(relay_sem, inc=1, device_id={"dp": z_peer(k) * CORES + core})

    @pl.when(me == 0)
    def _():
        for peer in seq_peers:
            pl.semaphore_signal(vouch_sem, inc=1, device_id={"seq": peer})

    for peer in seq_peers:
        send(send_ug.at[peer], recv_ug.at[me], 0, {"seq": peer})
    for peer in seq_peers:
        send(send_f.at[peer], recv_f.at[me], 1, {"seq": peer})
    recv_ug[me] = send_ug[me]
    recv_f[me] = send_f[me]

    loads[4].wait()
    pl.semaphore_wait(relay_sem, 2)
    pl.semaphore_signal(pair_sem, inc=1, device_id={"dp": z * CORES + other})

    @pl.when(me > 0)
    def _():
        pl.semaphore_wait(vouch_sem, 1)

    def transform(tiles_ref):
        lhs = jnp.concatenate(
            [tiles_ref[:, 0].reshape(2 * SEQ * OWN, HALF), tiles_ref[:, 1].reshape(2 * SEQ * OWN, HALF)], axis=1
        )
        return dot(lhs, w_ref[0], NN) + dot(lhs, w_ref[1], NN)

    await_bytes(recv_ug.at[pl.ds(0, SEQ - 1)], recv_sem, 0)
    spec[...] = transform(recv_ug).reshape(SEQ, 2, OWN, 2 * FREQ)

    lanes = lax.broadcasted_iota(jnp.int32, (OWN, FREQ), 1)
    sign = 1.0 - 2.0 * lax.rem(lanes, 2).astype(F32)
    for a in range(SEQ):
        re, im = spec[a, 1, :, :FREQ], spec[a, 1, :, FREQ:]
        if a < SEQ - 1:
            re, im = re + sign * spec[a + 1, 1, :, FREQ:], im - sign * spec[a + 1, 1, :, :FREQ]
        spin[a, :, :FREQ] = re
        spin[a, :, FREQ:] = im

    correlate(
        lambda a, lane: (
            spec[a, 0, :, lane : lane + HALF], spec[a, 0, :, FREQ + lane : FREQ + lane + HALF]
        ),
        spin, v_ref,
    )
    wide = dot(w_ref[0], v_ref[...], NT)
    weight = wide[:, :CH] + wide[:, CH:] + dot(w_ref[1], v_ref[0 : SEQ * OWN], NT)
    weight = weight * (1.0 / (PANEL * math.sqrt(CORES * ZED * SEQ * PANEL)))
    group = lax.div(lax.broadcasted_iota(jnp.int32, (2 * OWN, CH), 1), OWN)
    line = lax.broadcasted_iota(jnp.int32, (2 * OWN, CH), 0)

    for i, place in enumerate(EARLY):
        turned = pltpu.roll(weight[place * OWN : (place + 1) * OWN], 0, 1, stride=OWN, stride_axis=0)
        row = jnp.sum(jnp.where(group[:OWN] == line[:OWN], turned, 0.0), axis=0, keepdims=True)
        early_row[i : i + 1] = row
        here = early & (dp == place)

        @pl.when(here)
        def _():
            recv_early[pl.ds(dp * SEQ + me, 1)] = row

        @pl.when(jnp.logical_not(here))
        def _():
            send(
                early_row.at[pl.ds(i, 1)], recv_early.at[pl.ds(dp * SEQ + me, 1)], 6,
                {"seq": 0, "dp": place},
            )

    blocks = weight.reshape(ZED, CORES, OWN, CH)
    for side in range(CORES):
        part[side] = blocks[:, side]
    pl.semaphore_wait(pair_sem, 1)
    for i, k in enumerate(FAR):
        peer = z_peer(k)
        for side in range(CORES):
            send(part.at[side, peer], recv_far.at[i, core], 7, {"dp": peer * CORES + side})
    send(part.at[other], from_core, 2, {"dp": z * CORES + other})

    await_bytes(recv_f.at[pl.ds(0, SEQ - 1)], recv_sem, 1)
    both = transform(recv_f).reshape(SEQ, 2, OWN, 2 * FREQ)
    spec_f[...] = both[:, 0] + both[:, 1]

    await_bytes(from_core, recv_sem, 2)
    pair_sum[...] = part[core] + from_core[...]
    for i, k in enumerate(NEARER):
        peer = z_peer(k)
        send(pair_sum.at[peer], recv_z.at[i], 3, {"dp": peer * CORES + core})

    correlate(
        lambda a, lane: (spec_f[a, :, lane : lane + HALF], spec_f[a, :, FREQ + lane : FREQ + lane + HALF]),
        spin, v_ref,
    )
    tall = dot(v_ref[...], w_ref[0], NT)
    back = tall[: SEQ * OWN] + tall[SEQ * OWN :] + dot(v_ref[0 : SEQ * OWN], w_ref[1], NT)
    back = (back * (1.0 / PANEL)).reshape(SEQ, OWN, PANEL)
    send_in[...] = jnp.concatenate([back[:, :, :HALF], back[:, :, HALF:]], axis=1).astype(BF16)
    for peer in seq_peers:
        send(send_in.at[peer], recv_in.at[me], 4, {"seq": peer})
    recv_in[me] = send_in[me]

    await_bytes(recv_z, recv_sem, 3)
    await_bytes(recv_far, recv_sem, 7)
    far = recv_far[...].reshape(len(FAR) * CORES, OWN, CH)
    own_sum[...] = jnp.sum(recv_z[...], axis=0) + jnp.sum(far, axis=0) + pair_sum[z]
    @pl.when(early_dp)
    def _():
        for peer in seq_peers:
            @pl.when(peer > 0)
            def _():
                send(own_sum, recv_s.at[me], 5, {"seq": peer})

    @pl.when(jnp.logical_not(early_dp))
    def _():
        for peer in seq_peers:
            send(own_sum, recv_s.at[me], 5, {"seq": peer})

    recv_s[me] = own_sum[...]

    await_bytes(recv_in.at[pl.ds(0, SEQ - 1)], recv_sem, 4)
    for h in range(2):
        block = recv_in[...].astype(F32)[:, h * OWN : (h + 1) * OWN].reshape(CH, HALF)
        in_ref[0, h * HALF : (h + 1) * HALF] = block.T.astype(BF16)

    await_bytes(send_ug.at[pl.ds(0, SEQ - 1)], send_sem, 0)
    await_bytes(send_f.at[pl.ds(0, SEQ - 1)], send_sem, 1)
    await_bytes(from_core, send_sem, 2)
    await_bytes(recv_z, send_sem, 3)
    await_bytes(recv_far, send_sem, 7)
    await_bytes(send_in.at[pl.ds(0, SEQ - 1)], send_sem, 4)
    fewer = early_dp & (me > 0)

    @pl.when(fewer)
    def _():
        await_bytes(recv_s.at[pl.ds(0, SEQ - 2)], send_sem, 5)

    @pl.when(jnp.logical_not(fewer))
    def _():
        await_bytes(recv_s.at[pl.ds(0, SEQ - 1)], send_sem, 5)

    if len(EARLY) > 1:
        await_bytes(early_row.at[pl.ds(0, len(EARLY) - 1)], send_sem, 6)

    @pl.when(jnp.logical_not(early))
    def _():
        await_bytes(early_row.at[pl.ds(0, 1)], send_sem, 6)

    @pl.when(jnp.logical_not(early))
    def _():
        await_bytes(recv_s.at[pl.ds(0, SEQ - 1)], recv_sem, 5)
        result = jnp.zeros((OWN, CH), F32)
        for s in range(SEQ):
            turned = pltpu.roll(recv_s[s], lax.rem(s + SEQ - me, SEQ) * OWN, 1)
            result = jnp.where(group[:OWN] == s, turned, result)
        fg_ref[...] = result

    @pl.when(early)
    def _():
        await_bytes(recv_early.at[pl.ds(0, SEQ * CORES * ZED - 1)], recv_sem, 6)
        total = jnp.sum(recv_early[...].reshape(CORES * ZED, SEQ, CH), axis=0)
        turned = pltpu.roll(total, 0, 1, stride=OWN, stride_axis=0)
        for r in range(OWN):
            shifted = turned if r == 0 else pltpu.roll(turned, CH - r * OWN, 1)
            fg_ref[r : r + 1] = jnp.sum(jnp.where(group == line, shifted, 0.0), axis=0, keepdims=True)


def place(in_vmem, fg_vmem, in_hbm, fg_hbm, sem):
    copies = [
        pltpu.make_async_copy(in_vmem, in_hbm, sem.at[0]),
        pltpu.make_async_copy(fg_vmem, fg_hbm, sem.at[1]),
    ]
    for copy in copies:
        copy.start()
    for copy in copies:
        copy.wait()


def on_device(signal, out_grad, filt, skip):
    vmem = pl.BlockSpec(memory_space=pltpu.VMEM)
    operands = (signal, out_grad, filt, skip.reshape(1, CH), jnp.asarray(table()))
    tiles = (SEQ, 2, 2 * OWN, HALF)
    grads = pl.pallas_call(
        kernel,
        out_shape=(
            pltpu.VMEM((1, PANEL, CH), BF16),
            pltpu.VMEM((OWN, CH), F32),
        ),
        in_specs=[pl.BlockSpec(memory_space=pltpu.HBM)] * 5,
        out_specs=(vmem, vmem),
        scratch_shapes=[
            pltpu.VMEM((1, PANEL, CH), BF16),
            pltpu.VMEM((1, PANEL, CH), BF16),
            pltpu.VMEM((PANEL, CH), F32),
            pltpu.VMEM((1, CH), F32),
            pltpu.VMEM((2, PANEL, 2 * FREQ), BF16),
            pltpu.VMEM(tiles, BF16),
            pltpu.VMEM(tiles, BF16),
            pltpu.VMEM(tiles, BF16),
            pltpu.VMEM(tiles, BF16),
            pltpu.VMEM((SEQ, 2, OWN, 2 * FREQ), F32),
            pltpu.VMEM((SEQ, OWN, 2 * FREQ), F32),
            pltpu.VMEM((SEQ, OWN, 2 * FREQ), F32),
            pltpu.VMEM((2 * SEQ * OWN, 2 * FREQ), BF16),
            pltpu.VMEM((CORES, ZED, OWN, CH), F32),
            pltpu.VMEM((ZED, OWN, CH), F32),
            pltpu.VMEM((ZED, OWN, CH), F32),
            pltpu.VMEM((len(NEARER), OWN, CH), F32),
            pltpu.VMEM((OWN, CH), F32),
            pltpu.VMEM((SEQ, OWN, CH), F32),
            pltpu.VMEM((SEQ, 2 * OWN, HALF), BF16),
            pltpu.VMEM((SEQ, 2 * OWN, HALF), BF16),
            pltpu.SemaphoreType.DMA((8,)),
            pltpu.SemaphoreType.DMA((8,)),
            pltpu.SemaphoreType.DMA((5,)),
            pltpu.SemaphoreType.REGULAR,
            pltpu.SemaphoreType.REGULAR,
            pltpu.SemaphoreType.REGULAR,
            pltpu.VMEM((len(FAR), CORES, OWN, CH), F32),
            pltpu.VMEM((OWN, CH), F32),
            pltpu.VMEM((SEQ * CORES * ZED, CH), F32),
        ],
        compiler_params=pltpu.CompilerParams(
            collective_id=0, has_side_effects=True, vmem_limit_bytes=16 * 1024 * 1024
        ),
    )(*(pltpu.with_memory_space_constraint(x, pltpu.HBM) for x in operands))
    return pl.pallas_call(
        place,
        out_shape=(
            jax.ShapeDtypeStruct((1, PANEL, CH), BF16),
            jax.ShapeDtypeStruct((OWN, CH), F32),
        ),
        in_specs=[vmem] * 2,
        out_specs=(pl.BlockSpec(memory_space=pltpu.HBM),) * 2,
        scratch_shapes=[pltpu.SemaphoreType.DMA((2,))],
        compiler_params=pltpu.CompilerParams(vmem_limit_bytes=1024 * 1024),
    )(*grads)


def solution(mesh):
    placed = (P("dp", "seq", None), P("dp", "seq", None), P("seq", None), P())
    return jax.shard_map(
        on_device,
        mesh=mesh,
        in_specs=placed,
        out_specs=(P("dp", "seq", None), P(("seq", "dp"), None)),
        check_vma=False,
    )
```

```python
import functools
import math

import jax
import jax.numpy as jnp
import ml_dtypes
import numpy as np
from jax import lax
from jax.experimental import pallas as pl
from jax.experimental.pallas import tpu as pltpu
from jax.sharding import PartitionSpec as P

SEQ, ZED, CORES = 16, 16, 2
PANEL, HALF, CH, OWN = 256, 128, 128, 8
FREQ = PANEL
NEAR = 4
EARLY = ((0, 1), (1, 0), (4, 0), (1, 1), (4, 1), (0, 2), (0, 3))
COLUMNS = sorted({seq for seq, _ in EARLY})
SEQ_OFFSETS = sorted(
    ((i, j) for i in range(4) for j in range(4) if i + j), key=lambda o: -sum(min(k, 4 - k) for k in o)
)
Z_OFFSETS = sorted(range(1, ZED), key=lambda k: -min(k, ZED - k))
FAR, NEARER = Z_OFFSETS[:3], Z_OFFSETS[3:]
F32, BF16 = jnp.float32, jnp.bfloat16
NT = (((1,), (1,)), ((), ()))
NN = (((1,), (0,)), ((), ()))


def table():
    product = np.arange(PANEL)[:, None] * (2 * np.arange(FREQ)[None, :] + 1) % (4 * PANEL)
    phase = 2.0 * math.pi / (4 * PANEL) * product.astype(np.float64)
    full = np.concatenate([np.cos(phase), -np.sin(phase)], axis=1)
    high = full.astype(ml_dtypes.bfloat16)
    rest = (full - high.astype(np.float64)).astype(ml_dtypes.bfloat16)
    return np.stack([high, rest])


def dot(a, b, dims):
    return lax.dot_general(a, b, dims, preferred_element_type=F32)


def split(x):
    high = x.astype(BF16)
    return high, (x - high.astype(F32)).astype(BF16)


def correlate(x_of, g_ref, v_ref):
    for lane in range(0, FREQ, HALF):
        total_re = total_im = None
        for a in range(SEQ):
            x_re, x_im = x_of(a, lane)
            g_re = g_ref[a:, :, lane : lane + HALF]
            g_im = g_ref[a:, :, FREQ + lane : FREQ + lane + HALF]
            new_re = x_re * g_re + x_im * g_im
            new_im = x_re * g_im - x_im * g_re
            if a == 0:
                total_re, total_im = new_re, new_im
            else:
                n = SEQ - a
                total_re = jnp.concatenate([total_re[:n] + new_re, total_re[n:]], axis=0)
                total_im = jnp.concatenate([total_im[:n] + new_im, total_im[n:]], axis=0)
        for total, first in ((total_re, lane), (total_im, FREQ + lane)):
            high, rest = split(total.reshape(SEQ * OWN, HALF))
            v_ref[0 : SEQ * OWN, first : first + HALF] = high
            v_ref[SEQ * OWN :, first : first + HALF] = rest


def beside(dp, place):
    near = min((dp // CORES - place // CORES) % ZED, (place // CORES - dp // CORES) % ZED)
    return near == 0 or (near <= NEAR and dp % CORES == place % CORES)


def kernel(
    u_hbm, g_hbm, f_hbm, skip_hbm, w_hbm, in_ref, fg_ref,
    u_ref, g_ref, f_ref, skip_ref, w_ref, send_ug, recv_ug, send_f, recv_f, spec, spec_f, spin, v_ref, part, from_core, pair_sum, recv_z,
    own_sum, recv_s, send_in, recv_in, send_sem, recv_sem, load_sem, relay_sem, vouch_sem, pair_sem, recv_far, early_row, recv_early,
):
    me, dp = lax.axis_index("seq"), lax.axis_index("dp")
    z, core = lax.div(dp, CORES), lax.rem(dp, CORES)
    x, y = lax.div(me, 4), lax.rem(me, 4)
    seq_peers = [lax.rem(x + i, 4) * 4 + lax.rem(y + j, 4) for i, j in SEQ_OFFSETS]
    z_peer = lambda k: lax.rem(z + k, ZED)
    other = 1 - core

    loads = [
        pltpu.make_async_copy(src, dst, load_sem.at[i])
        for i, (src, dst) in enumerate(
            ((u_hbm, u_ref), (g_hbm, g_ref), (f_hbm, f_ref), (skip_hbm, skip_ref), (w_hbm, w_ref))
        )
    ]
    for load in loads[:2]:
        load.start()
    barrier = pltpu.get_barrier_semaphore()
    for k in Z_OFFSETS[-2 * NEAR :]:
        pl.semaphore_signal(barrier, inc=1, device_id={"dp": z_peer(k) * CORES + core})
    for peer in seq_peers:
        pl.semaphore_signal(barrier, inc=1, device_id={"seq": peer})
    pl.semaphore_signal(barrier, inc=1, device_id={"dp": z * CORES + other})

    for load in loads[2:]:
        load.start()

    any_of = lambda terms: functools.reduce(jnp.logical_or, terms)
    early = any_of([(me == seq) & (dp == place) for seq, place in EARLY])
    early_dp = any_of([dp == place for place in sorted({place for _, place in EARLY})])
    in_column = any_of([me == seq for seq in COLUMNS])
    greetings = SEQ + 2 * NEAR
    for seq, place in EARLY:
        strangers = [k for k in range(CORES * ZED) if not beside(k, place)]
        greetings += jnp.where((me == seq) & any_of([dp == k for k in strangers]), 1, 0)

        @pl.when((me == seq) & (dp == place))
        def _():
            for k in strangers:
                pl.semaphore_signal(barrier, inc=1, device_id={"dp": k})

    def send(src, dst, place, device):
        pltpu.make_async_remote_copy(
            src_ref=src, dst_ref=dst, send_sem=send_sem.at[place], recv_sem=recv_sem.at[place], device_id=device
        ).start()

    def await_bytes(ref, sem, place):
        pltpu.make_async_copy(ref, ref, sem.at[place]).wait()

    rows = lax.broadcasted_iota(jnp.int32, (CH, CH), 0)
    eye = (rows == lax.broadcasted_iota(jnp.int32, (CH, CH), 1)).astype(F32).astype(BF16)

    def stage(first, second, out_ref):
        first, second = dot(eye, first, NT), dot(eye, second, NT)
        for h in range(2):
            lanes = slice(h * HALF, (h + 1) * HALF)
            tile = jnp.concatenate(
                [first[:, lanes].reshape(SEQ, OWN, HALF), second[:, lanes].reshape(SEQ, OWN, HALF)], axis=1
            )
            out_ref[:, h] = tile.astype(BF16)

    loads[0].wait()
    loads[1].wait()
    stage(u_ref[0], g_ref[0], send_ug)
    loads[2].wait()
    loads[3].wait()
    tap = lax.broadcasted_iota(jnp.int32, (PANEL, CH), 0) + me
    filt = f_ref[...] + jnp.where(tap == 0, jnp.broadcast_to(skip_ref[...], (PANEL, CH)), 0.0)
    stage(*split(filt), send_f)

    pl.semaphore_wait(barrier, greetings)
    for k in (NEAR, ZED - NEAR):
        pl.semaphore_signal(relay_sem, inc=1, device_id={"dp": z_peer(k) * CORES + core})

    @pl.when(in_column)
    def _():
        for peer in seq_peers:
            pl.semaphore_signal(vouch_sem, inc=1, device_id={"seq": peer})

    for peer in seq_peers:
        send(send_ug.at[peer], recv_ug.at[me], 0, {"seq": peer})
    for peer in seq_peers:
        send(send_f.at[peer], recv_f.at[me], 1, {"seq": peer})
    recv_ug[me] = send_ug[me]
    recv_f[me] = send_f[me]

    loads[4].wait()
    pl.semaphore_wait(relay_sem, 2)
    pl.semaphore_signal(pair_sem, inc=1, device_id={"dp": z * CORES + other})

    pl.semaphore_wait(vouch_sem, jnp.where(in_column, len(COLUMNS) - 1, len(COLUMNS)))

    def transform(tiles_ref):
        lhs = jnp.concatenate(
            [tiles_ref[:, 0].reshape(2 * SEQ * OWN, HALF), tiles_ref[:, 1].reshape(2 * SEQ * OWN, HALF)], axis=1
        )
        return dot(lhs, w_ref[0], NN) + dot(lhs, w_ref[1], NN)

    await_bytes(recv_ug.at[pl.ds(0, SEQ - 1)], recv_sem, 0)
    spec[...] = transform(recv_ug).reshape(SEQ, 2, OWN, 2 * FREQ)

    lanes = lax.broadcasted_iota(jnp.int32, (OWN, FREQ), 1)
    sign = 1.0 - 2.0 * lax.rem(lanes, 2).astype(F32)
    for a in range(SEQ):
        re, im = spec[a, 1, :, :FREQ], spec[a, 1, :, FREQ:]
        if a < SEQ - 1:
            re, im = re + sign * spec[a + 1, 1, :, FREQ:], im - sign * spec[a + 1, 1, :, :FREQ]
        spin[a, :, :FREQ] = re
        spin[a, :, FREQ:] = im

    correlate(
        lambda a, lane: (
            spec[a, 0, :, lane : lane + HALF], spec[a, 0, :, FREQ + lane : FREQ + lane + HALF]
        ),
        spin, v_ref,
    )
    wide = dot(w_ref[0], v_ref[...], NT)
    weight = wide[:, :CH] + wide[:, CH:] + dot(w_ref[1], v_ref[0 : SEQ * OWN], NT)
    weight = weight * (1.0 / (PANEL * math.sqrt(CORES * ZED * SEQ * PANEL)))
    group = lax.div(lax.broadcasted_iota(jnp.int32, (2 * OWN, CH), 1), OWN)
    line = lax.broadcasted_iota(jnp.int32, (2 * OWN, CH), 0)

    for i, (seq, place) in enumerate(EARLY):
        turned = pltpu.roll(weight[place * OWN : (place + 1) * OWN], 0, 1, stride=OWN, stride_axis=0)
        place_of = lax.rem(line[:OWN] + seq, SEQ)
        row = jnp.sum(jnp.where(group[:OWN] == place_of, turned, 0.0), axis=0, keepdims=True)
        early_row[i : i + 1] = row
        here = (me == seq) & (dp == place)

        @pl.when(here)
        def _():
            recv_early[pl.ds(dp * SEQ + me, 1)] = row

        @pl.when(jnp.logical_not(here))
        def _():
            send(
                early_row.at[pl.ds(i, 1)], recv_early.at[pl.ds(dp * SEQ + me, 1)], 6,
                {"seq": seq, "dp": place},
            )

    blocks = weight.reshape(ZED, CORES, OWN, CH)
    for side in range(CORES):
        part[side] = blocks[:, side]
    pl.semaphore_wait(pair_sem, 1)
    for i, k in enumerate(FAR):
        peer = z_peer(k)
        for side in range(CORES):
            send(part.at[side, peer], recv_far.at[i, core], 7, {"dp": peer * CORES + side})
    send(part.at[other], from_core, 2, {"dp": z * CORES + other})

    await_bytes(recv_f.at[pl.ds(0, SEQ - 1)], recv_sem, 1)
    both = transform(recv_f).reshape(SEQ, 2, OWN, 2 * FREQ)
    spec_f[...] = both[:, 0] + both[:, 1]

    await_bytes(from_core, recv_sem, 2)
    pair_sum[...] = part[core] + from_core[...]
    for i, k in enumerate(NEARER):
        peer = z_peer(k)
        send(pair_sum.at[peer], recv_z.at[i], 3, {"dp": peer * CORES + core})

    correlate(
        lambda a, lane: (spec_f[a, :, lane : lane + HALF], spec_f[a, :, FREQ + lane : FREQ + lane + HALF]),
        spin, v_ref,
    )
    tall = dot(v_ref[...], w_ref[0], NT)
    back = tall[: SEQ * OWN] + tall[SEQ * OWN :] + dot(v_ref[0 : SEQ * OWN], w_ref[1], NT)
    back = (back * (1.0 / PANEL)).reshape(SEQ, OWN, PANEL)
    send_in[...] = jnp.concatenate([back[:, :, :HALF], back[:, :, HALF:]], axis=1).astype(BF16)
    for peer in seq_peers:
        send(send_in.at[peer], recv_in.at[me], 4, {"seq": peer})
    recv_in[me] = send_in[me]

    await_bytes(recv_z, recv_sem, 3)
    await_bytes(recv_far, recv_sem, 7)
    far = recv_far[...].reshape(len(FAR) * CORES, OWN, CH)
    own_sum[...] = jnp.sum(recv_z[...], axis=0) + jnp.sum(far, axis=0) + pair_sum[z]
    @pl.when(early_dp)
    def _():
        for peer in seq_peers:
            direct = any_of([(peer == seq) & (dp == place) for seq, place in EARLY])

            @pl.when(jnp.logical_not(direct))
            def _():
                send(own_sum, recv_s.at[me], 5, {"seq": peer})

    @pl.when(jnp.logical_not(early_dp))
    def _():
        for peer in seq_peers:
            send(own_sum, recv_s.at[me], 5, {"seq": peer})

    recv_s[me] = own_sum[...]

    await_bytes(recv_in.at[pl.ds(0, SEQ - 1)], recv_sem, 4)
    for h in range(2):
        block = recv_in[...].astype(F32)[:, h * OWN : (h + 1) * OWN].reshape(CH, HALF)
        in_ref[0, h * HALF : (h + 1) * HALF] = block.T.astype(BF16)

    await_bytes(send_ug.at[pl.ds(0, SEQ - 1)], send_sem, 0)
    await_bytes(send_f.at[pl.ds(0, SEQ - 1)], send_sem, 1)
    await_bytes(from_core, send_sem, 2)
    await_bytes(recv_z, send_sem, 3)
    await_bytes(recv_far, send_sem, 7)
    await_bytes(send_in.at[pl.ds(0, SEQ - 1)], send_sem, 4)
    sent = SEQ - 1
    for seq, place in EARLY:
        sent -= jnp.where((dp == place) & (me != seq), 1, 0)

    def sent_one(i, carry):
        await_bytes(own_sum, send_sem, 5)
        return carry

    lax.fori_loop(0, sent, sent_one, 0)
    for seq, place in EARLY:
        @pl.when(jnp.logical_not((me == seq) & (dp == place)))
        def _():
            await_bytes(early_row.at[pl.ds(0, 1)], send_sem, 6)

    @pl.when(jnp.logical_not(early))
    def _():
        await_bytes(recv_s.at[pl.ds(0, SEQ - 1)], recv_sem, 5)
        result = jnp.zeros((OWN, CH), F32)
        for s in range(SEQ):
            turned = pltpu.roll(recv_s[s], lax.rem(s + SEQ - me, SEQ) * OWN, 1)
            result = jnp.where(group[:OWN] == s, turned, result)
        fg_ref[...] = result

    @pl.when(early)
    def _():
        await_bytes(recv_early.at[pl.ds(0, SEQ * CORES * ZED - 1)], recv_sem, 6)
        total = jnp.sum(recv_early[...].reshape(CORES * ZED, SEQ, CH), axis=0)
        total = pltpu.roll(total, (SEQ - me) * OWN, 1)
        turned = pltpu.roll(total, 0, 1, stride=OWN, stride_axis=0)
        for r in range(OWN):
            shifted = turned if r == 0 else pltpu.roll(turned, CH - r * OWN, 1)
            fg_ref[r : r + 1] = jnp.sum(jnp.where(group == line, shifted, 0.0), axis=0, keepdims=True)


def place(in_vmem, fg_vmem, in_hbm, fg_hbm, sem):
    copies = [
        pltpu.make_async_copy(in_vmem, in_hbm, sem.at[0]),
        pltpu.make_async_copy(fg_vmem, fg_hbm, sem.at[1]),
    ]
    for copy in copies:
        copy.start()
    for copy in copies:
        copy.wait()


def on_device(signal, out_grad, filt, skip):
    vmem = pl.BlockSpec(memory_space=pltpu.VMEM)
    operands = (signal, out_grad, filt, skip.reshape(1, CH), jnp.asarray(table()))
    tiles = (SEQ, 2, 2 * OWN, HALF)
    grads = pl.pallas_call(
        kernel,
        out_shape=(
            pltpu.VMEM((1, PANEL, CH), BF16),
            pltpu.VMEM((OWN, CH), F32),
        ),
        in_specs=[pl.BlockSpec(memory_space=pltpu.HBM)] * 5,
        out_specs=(vmem, vmem),
        scratch_shapes=[
            pltpu.VMEM((1, PANEL, CH), BF16),
            pltpu.VMEM((1, PANEL, CH), BF16),
            pltpu.VMEM((PANEL, CH), F32),
            pltpu.VMEM((1, CH), F32),
            pltpu.VMEM((2, PANEL, 2 * FREQ), BF16),
            pltpu.VMEM(tiles, BF16),
            pltpu.VMEM(tiles, BF16),
            pltpu.VMEM(tiles, BF16),
            pltpu.VMEM(tiles, BF16),
            pltpu.VMEM((SEQ, 2, OWN, 2 * FREQ), F32),
            pltpu.VMEM((SEQ, OWN, 2 * FREQ), F32),
            pltpu.VMEM((SEQ, OWN, 2 * FREQ), F32),
            pltpu.VMEM((2 * SEQ * OWN, 2 * FREQ), BF16),
            pltpu.VMEM((CORES, ZED, OWN, CH), F32),
            pltpu.VMEM((ZED, OWN, CH), F32),
            pltpu.VMEM((ZED, OWN, CH), F32),
            pltpu.VMEM((len(NEARER), OWN, CH), F32),
            pltpu.VMEM((OWN, CH), F32),
            pltpu.VMEM((SEQ, OWN, CH), F32),
            pltpu.VMEM((SEQ, 2 * OWN, HALF), BF16),
            pltpu.VMEM((SEQ, 2 * OWN, HALF), BF16),
            pltpu.SemaphoreType.DMA((8,)),
            pltpu.SemaphoreType.DMA((8,)),
            pltpu.SemaphoreType.DMA((5,)),
            pltpu.SemaphoreType.REGULAR,
            pltpu.SemaphoreType.REGULAR,
            pltpu.SemaphoreType.REGULAR,
            pltpu.VMEM((len(FAR), CORES, OWN, CH), F32),
            pltpu.VMEM((2 * OWN, CH), F32),
            pltpu.VMEM((SEQ * CORES * ZED, CH), F32),
        ],
        compiler_params=pltpu.CompilerParams(
            collective_id=0, has_side_effects=True, vmem_limit_bytes=16 * 1024 * 1024
        ),
    )(*(pltpu.with_memory_space_constraint(x, pltpu.HBM) for x in operands))
    return pl.pallas_call(
        place,
        out_shape=(
            jax.ShapeDtypeStruct((1, PANEL, CH), BF16),
            jax.ShapeDtypeStruct((OWN, CH), F32),
        ),
        in_specs=[vmem] * 2,
        out_specs=(pl.BlockSpec(memory_space=pltpu.HBM),) * 2,
        scratch_shapes=[pltpu.SemaphoreType.DMA((2,))],
        compiler_params=pltpu.CompilerParams(vmem_limit_bytes=1024 * 1024),
    )(*grads)


def solution(mesh):
    placed = (P("dp", "seq", None), P("dp", "seq", None), P("seq", None), P())
    return jax.shard_map(
        on_device,
        mesh=mesh,
        in_specs=placed,
        out_specs=(P("dp", "seq", None), P(("seq", "dp"), None)),
        check_vma=False,
    )
```

```python
import functools
import math

import jax
import jax.numpy as jnp
import ml_dtypes
import numpy as np
from jax import lax
from jax.experimental import pallas as pl
from jax.experimental.pallas import tpu as pltpu
from jax.sharding import PartitionSpec as P

SEQ, ZED, CORES = 16, 16, 2
PANEL, HALF, CH, OWN = 256, 128, 128, 8
FREQ = PANEL
NEAR = 4
EARLY = ((0, 1), (1, 0), (4, 0), (1, 1), (4, 1), (0, 2), (0, 3), (8, 0), (8, 1), (12, 0), (12, 1))
COLUMNS = sorted({seq for seq, _ in EARLY})
SEQ_OFFSETS = sorted(
    ((i, j) for i in range(4) for j in range(4) if i + j), key=lambda o: -sum(min(k, 4 - k) for k in o)
)
Z_OFFSETS = sorted(range(1, ZED), key=lambda k: -min(k, ZED - k))
FAR, NEARER = Z_OFFSETS[:3], Z_OFFSETS[3:]
F32, BF16 = jnp.float32, jnp.bfloat16
NT = (((1,), (1,)), ((), ()))
NN = (((1,), (0,)), ((), ()))


def table():
    product = np.arange(PANEL)[:, None] * (2 * np.arange(FREQ)[None, :] + 1) % (4 * PANEL)
    phase = 2.0 * math.pi / (4 * PANEL) * product.astype(np.float64)
    full = np.concatenate([np.cos(phase), -np.sin(phase)], axis=1)
    high = full.astype(ml_dtypes.bfloat16)
    rest = (full - high.astype(np.float64)).astype(ml_dtypes.bfloat16)
    return np.stack([high, rest])


def dot(a, b, dims):
    return lax.dot_general(a, b, dims, preferred_element_type=F32)


def split(x):
    high = x.astype(BF16)
    return high, (x - high.astype(F32)).astype(BF16)


def correlate(x_of, g_ref, v_ref):
    for lane in range(0, FREQ, HALF):
        total_re = total_im = None
        for a in range(SEQ):
            x_re, x_im = x_of(a, lane)
            g_re = g_ref[a:, :, lane : lane + HALF]
            g_im = g_ref[a:, :, FREQ + lane : FREQ + lane + HALF]
            new_re = x_re * g_re + x_im * g_im
            new_im = x_re * g_im - x_im * g_re
            if a == 0:
                total_re, total_im = new_re, new_im
            else:
                n = SEQ - a
                total_re = jnp.concatenate([total_re[:n] + new_re, total_re[n:]], axis=0)
                total_im = jnp.concatenate([total_im[:n] + new_im, total_im[n:]], axis=0)
        for total, first in ((total_re, lane), (total_im, FREQ + lane)):
            high, rest = split(total.reshape(SEQ * OWN, HALF))
            v_ref[0 : SEQ * OWN, first : first + HALF] = high
            v_ref[SEQ * OWN :, first : first + HALF] = rest


def beside(dp, place):
    near = min((dp // CORES - place // CORES) % ZED, (place // CORES - dp // CORES) % ZED)
    return near == 0 or (near <= NEAR and dp % CORES == place % CORES)


def kernel(
    u_hbm, g_hbm, f_hbm, skip_hbm, w_hbm, in_ref, fg_ref,
    u_ref, g_ref, f_ref, skip_ref, w_ref, send_ug, recv_ug, send_f, recv_f, spec, spec_f, spin, v_ref, part, from_core, pair_sum, recv_z,
    own_sum, recv_s, send_in, recv_in, send_sem, recv_sem, load_sem, relay_sem, vouch_sem, pair_sem, recv_far, early_row, recv_early,
):
    me, dp = lax.axis_index("seq"), lax.axis_index("dp")
    z, core = lax.div(dp, CORES), lax.rem(dp, CORES)
    x, y = lax.div(me, 4), lax.rem(me, 4)
    seq_peers = [lax.rem(x + i, 4) * 4 + lax.rem(y + j, 4) for i, j in SEQ_OFFSETS]
    z_peer = lambda k: lax.rem(z + k, ZED)
    other = 1 - core

    loads = [
        pltpu.make_async_copy(src, dst, load_sem.at[i])
        for i, (src, dst) in enumerate(
            ((u_hbm, u_ref), (g_hbm, g_ref), (f_hbm, f_ref), (skip_hbm, skip_ref), (w_hbm, w_ref))
        )
    ]
    for load in loads[:2]:
        load.start()
    barrier = pltpu.get_barrier_semaphore()
    for k in Z_OFFSETS[-2 * NEAR :]:
        pl.semaphore_signal(barrier, inc=1, device_id={"dp": z_peer(k) * CORES + core})
    for peer in seq_peers:
        pl.semaphore_signal(barrier, inc=1, device_id={"seq": peer})
    pl.semaphore_signal(barrier, inc=1, device_id={"dp": z * CORES + other})

    for load in loads[2:]:
        load.start()

    any_of = lambda terms: functools.reduce(jnp.logical_or, terms)
    early = any_of([(me == seq) & (dp == place) for seq, place in EARLY])
    early_dp = any_of([dp == place for place in sorted({place for _, place in EARLY})])
    in_column = any_of([me == seq for seq in COLUMNS])
    greetings = SEQ + 2 * NEAR
    for seq, place in EARLY:
        strangers = [k for k in range(CORES * ZED) if not beside(k, place)]
        greetings += jnp.where((me == seq) & any_of([dp == k for k in strangers]), 1, 0)

        @pl.when((me == seq) & (dp == place))
        def _():
            for k in strangers:
                pl.semaphore_signal(barrier, inc=1, device_id={"dp": k})

    def send(src, dst, place, device):
        pltpu.make_async_remote_copy(
            src_ref=src, dst_ref=dst, send_sem=send_sem.at[place], recv_sem=recv_sem.at[place], device_id=device
        ).start()

    def await_bytes(ref, sem, place):
        pltpu.make_async_copy(ref, ref, sem.at[place]).wait()

    rows = lax.broadcasted_iota(jnp.int32, (CH, CH), 0)
    eye = (rows == lax.broadcasted_iota(jnp.int32, (CH, CH), 1)).astype(F32).astype(BF16)

    def stage(first, second, out_ref):
        first, second = dot(eye, first, NT), dot(eye, second, NT)
        for h in range(2):
            lanes = slice(h * HALF, (h + 1) * HALF)
            tile = jnp.concatenate(
                [first[:, lanes].reshape(SEQ, OWN, HALF), second[:, lanes].reshape(SEQ, OWN, HALF)], axis=1
            )
            out_ref[:, h] = tile.astype(BF16)

    loads[0].wait()
    loads[1].wait()
    stage(u_ref[0], g_ref[0], send_ug)
    loads[2].wait()
    loads[3].wait()
    tap = lax.broadcasted_iota(jnp.int32, (PANEL, CH), 0) + me
    filt = f_ref[...] + jnp.where(tap == 0, jnp.broadcast_to(skip_ref[...], (PANEL, CH)), 0.0)
    stage(*split(filt), send_f)

    pl.semaphore_wait(barrier, greetings)
    for k in (NEAR, ZED - NEAR):
        pl.semaphore_signal(relay_sem, inc=1, device_id={"dp": z_peer(k) * CORES + core})

    @pl.when(in_column)
    def _():
        for peer in seq_peers:
            pl.semaphore_signal(vouch_sem, inc=1, device_id={"seq": peer})

    for peer in seq_peers:
        send(send_ug.at[peer], recv_ug.at[me], 0, {"seq": peer})
    for peer in seq_peers:
        send(send_f.at[peer], recv_f.at[me], 1, {"seq": peer})
    recv_ug[me] = send_ug[me]
    recv_f[me] = send_f[me]

    loads[4].wait()
    pl.semaphore_wait(relay_sem, 2)
    pl.semaphore_signal(pair_sem, inc=1, device_id={"dp": z * CORES + other})

    pl.semaphore_wait(vouch_sem, jnp.where(in_column, len(COLUMNS) - 1, len(COLUMNS)))

    def transform(tiles_ref):
        lhs = jnp.concatenate(
            [tiles_ref[:, 0].reshape(2 * SEQ * OWN, HALF), tiles_ref[:, 1].reshape(2 * SEQ * OWN, HALF)], axis=1
        )
        return dot(lhs, w_ref[0], NN) + dot(lhs, w_ref[1], NN)

    await_bytes(recv_ug.at[pl.ds(0, SEQ - 1)], recv_sem, 0)
    spec[...] = transform(recv_ug).reshape(SEQ, 2, OWN, 2 * FREQ)

    lanes = lax.broadcasted_iota(jnp.int32, (OWN, FREQ), 1)
    sign = 1.0 - 2.0 * lax.rem(lanes, 2).astype(F32)
    for a in range(SEQ):
        re, im = spec[a, 1, :, :FREQ], spec[a, 1, :, FREQ:]
        if a < SEQ - 1:
            re, im = re + sign * spec[a + 1, 1, :, FREQ:], im - sign * spec[a + 1, 1, :, :FREQ]
        spin[a, :, :FREQ] = re
        spin[a, :, FREQ:] = im

    correlate(
        lambda a, lane: (
            spec[a, 0, :, lane : lane + HALF], spec[a, 0, :, FREQ + lane : FREQ + lane + HALF]
        ),
        spin, v_ref,
    )
    wide = dot(w_ref[0], v_ref[...], NT)
    weight = wide[:, :CH] + wide[:, CH:] + dot(w_ref[1], v_ref[0 : SEQ * OWN], NT)
    weight = weight * (1.0 / (PANEL * math.sqrt(CORES * ZED * SEQ * PANEL)))
    group = lax.div(lax.broadcasted_iota(jnp.int32, (2 * OWN, CH), 1), OWN)
    line = lax.broadcasted_iota(jnp.int32, (2 * OWN, CH), 0)

    def tell(i):
        seq, place = EARLY[i]
        turned = pltpu.roll(weight[place * OWN : (place + 1) * OWN], 0, 1, stride=OWN, stride_axis=0)
        place_of = lax.rem(line[:OWN] + seq, SEQ)
        row = jnp.sum(jnp.where(group[:OWN] == place_of, turned, 0.0), axis=0, keepdims=True)
        early_row[i : i + 1] = row
        here = (me == seq) & (dp == place)

        @pl.when(here)
        def _():
            recv_early[pl.ds(dp * SEQ + me, 1)] = row

        @pl.when(jnp.logical_not(here))
        def _():
            send(
                early_row.at[pl.ds(i, 1)], recv_early.at[pl.ds(dp * SEQ + me, 1)], 6,
                {"seq": seq, "dp": place},
            )

    tell(0)
    blocks = weight.reshape(ZED, CORES, OWN, CH)
    for side in range(CORES):
        part[side] = blocks[:, side]
    pl.semaphore_wait(pair_sem, 1)
    for i, k in enumerate(FAR):
        peer = z_peer(k)
        for side in range(CORES):
            send(part.at[side, peer], recv_far.at[i, core], 7, {"dp": peer * CORES + side})
    send(part.at[other], from_core, 2, {"dp": z * CORES + other})
    for i in range(1, len(EARLY)):
        tell(i)

    await_bytes(recv_f.at[pl.ds(0, SEQ - 1)], recv_sem, 1)
    both = transform(recv_f).reshape(SEQ, 2, OWN, 2 * FREQ)
    spec_f[...] = both[:, 0] + both[:, 1]

    await_bytes(from_core, recv_sem, 2)
    pair_sum[...] = part[core] + from_core[...]
    for i, k in enumerate(NEARER):
        peer = z_peer(k)
        send(pair_sum.at[peer], recv_z.at[i], 3, {"dp": peer * CORES + core})

    correlate(
        lambda a, lane: (spec_f[a, :, lane : lane + HALF], spec_f[a, :, FREQ + lane : FREQ + lane + HALF]),
        spin, v_ref,
    )
    tall = dot(v_ref[...], w_ref[0], NT)
    back = tall[: SEQ * OWN] + tall[SEQ * OWN :] + dot(v_ref[0 : SEQ * OWN], w_ref[1], NT)
    back = (back * (1.0 / PANEL)).reshape(SEQ, OWN, PANEL)
    send_in[...] = jnp.concatenate([back[:, :, :HALF], back[:, :, HALF:]], axis=1).astype(BF16)
    for peer in seq_peers:
        send(send_in.at[peer], recv_in.at[me], 4, {"seq": peer})
    recv_in[me] = send_in[me]

    await_bytes(recv_z, recv_sem, 3)
    await_bytes(recv_far, recv_sem, 7)
    far = recv_far[...].reshape(len(FAR) * CORES, OWN, CH)
    own_sum[...] = jnp.sum(recv_z[...], axis=0) + jnp.sum(far, axis=0) + pair_sum[z]
    @pl.when(early_dp)
    def _():
        for peer in seq_peers:
            direct = any_of([(peer == seq) & (dp == place) for seq, place in EARLY])

            @pl.when(jnp.logical_not(direct))
            def _():
                send(own_sum, recv_s.at[me], 5, {"seq": peer})

    @pl.when(jnp.logical_not(early_dp))
    def _():
        for peer in seq_peers:
            send(own_sum, recv_s.at[me], 5, {"seq": peer})

    recv_s[me] = own_sum[...]

    await_bytes(recv_in.at[pl.ds(0, SEQ - 1)], recv_sem, 4)
    for h in range(2):
        block = recv_in[...].astype(F32)[:, h * OWN : (h + 1) * OWN].reshape(CH, HALF)
        in_ref[0, h * HALF : (h + 1) * HALF] = block.T.astype(BF16)

    await_bytes(send_ug.at[pl.ds(0, SEQ - 1)], send_sem, 0)
    await_bytes(send_f.at[pl.ds(0, SEQ - 1)], send_sem, 1)
    await_bytes(from_core, send_sem, 2)
    await_bytes(recv_z, send_sem, 3)
    await_bytes(recv_far, send_sem, 7)
    await_bytes(send_in.at[pl.ds(0, SEQ - 1)], send_sem, 4)
    sent = SEQ - 1
    for seq, place in EARLY:
        sent -= jnp.where((dp == place) & (me != seq), 1, 0)

    def sent_one(i, carry):
        await_bytes(own_sum, send_sem, 5)
        return carry

    lax.fori_loop(0, sent, sent_one, 0)
    for seq, place in EARLY:
        @pl.when(jnp.logical_not((me == seq) & (dp == place)))
        def _():
            await_bytes(early_row.at[pl.ds(0, 1)], send_sem, 6)

    @pl.when(jnp.logical_not(early))
    def _():
        await_bytes(recv_s.at[pl.ds(0, SEQ - 1)], recv_sem, 5)
        result = jnp.zeros((OWN, CH), F32)
        for s in range(SEQ):
            turned = pltpu.roll(recv_s[s], lax.rem(s + SEQ - me, SEQ) * OWN, 1)
            result = jnp.where(group[:OWN] == s, turned, result)
        fg_ref[...] = result

    @pl.when(early)
    def _():
        await_bytes(recv_early.at[pl.ds(0, SEQ * CORES * ZED - 1)], recv_sem, 6)
        total = jnp.sum(recv_early[...].reshape(CORES * ZED, SEQ, CH), axis=0)
        total = pltpu.roll(total, (SEQ - me) * OWN, 1)
        turned = pltpu.roll(total, 0, 1, stride=OWN, stride_axis=0)
        for r in range(OWN):
            shifted = turned if r == 0 else pltpu.roll(turned, CH - r * OWN, 1)
            fg_ref[r : r + 1] = jnp.sum(jnp.where(group == line, shifted, 0.0), axis=0, keepdims=True)


def place(in_vmem, fg_vmem, in_hbm, fg_hbm, sem):
    copies = [
        pltpu.make_async_copy(in_vmem, in_hbm, sem.at[0]),
        pltpu.make_async_copy(fg_vmem, fg_hbm, sem.at[1]),
    ]
    for copy in copies:
        copy.start()
    for copy in copies:
        copy.wait()


def on_device(signal, out_grad, filt, skip):
    vmem = pl.BlockSpec(memory_space=pltpu.VMEM)
    operands = (signal, out_grad, filt, skip.reshape(1, CH), jnp.asarray(table()))
    tiles = (SEQ, 2, 2 * OWN, HALF)
    grads = pl.pallas_call(
        kernel,
        out_shape=(
            pltpu.VMEM((1, PANEL, CH), BF16),
            pltpu.VMEM((OWN, CH), F32),
        ),
        in_specs=[pl.BlockSpec(memory_space=pltpu.HBM)] * 5,
        out_specs=(vmem, vmem),
        scratch_shapes=[
            pltpu.VMEM((1, PANEL, CH), BF16),
            pltpu.VMEM((1, PANEL, CH), BF16),
            pltpu.VMEM((PANEL, CH), F32),
            pltpu.VMEM((1, CH), F32),
            pltpu.VMEM((2, PANEL, 2 * FREQ), BF16),
            pltpu.VMEM(tiles, BF16),
            pltpu.VMEM(tiles, BF16),
            pltpu.VMEM(tiles, BF16),
            pltpu.VMEM(tiles, BF16),
            pltpu.VMEM((SEQ, 2, OWN, 2 * FREQ), F32),
            pltpu.VMEM((SEQ, OWN, 2 * FREQ), F32),
            pltpu.VMEM((SEQ, OWN, 2 * FREQ), F32),
            pltpu.VMEM((2 * SEQ * OWN, 2 * FREQ), BF16),
            pltpu.VMEM((CORES, ZED, OWN, CH), F32),
            pltpu.VMEM((ZED, OWN, CH), F32),
            pltpu.VMEM((ZED, OWN, CH), F32),
            pltpu.VMEM((len(NEARER), OWN, CH), F32),
            pltpu.VMEM((OWN, CH), F32),
            pltpu.VMEM((SEQ, OWN, CH), F32),
            pltpu.VMEM((SEQ, 2 * OWN, HALF), BF16),
            pltpu.VMEM((SEQ, 2 * OWN, HALF), BF16),
            pltpu.SemaphoreType.DMA((8,)),
            pltpu.SemaphoreType.DMA((8,)),
            pltpu.SemaphoreType.DMA((5,)),
            pltpu.SemaphoreType.REGULAR,
            pltpu.SemaphoreType.REGULAR,
            pltpu.SemaphoreType.REGULAR,
            pltpu.VMEM((len(FAR), CORES, OWN, CH), F32),
            pltpu.VMEM((4 * OWN, CH), F32),
            pltpu.VMEM((SEQ * CORES * ZED, CH), F32),
        ],
        compiler_params=pltpu.CompilerParams(
            collective_id=0, has_side_effects=True, vmem_limit_bytes=16 * 1024 * 1024
        ),
    )(*(pltpu.with_memory_space_constraint(x, pltpu.HBM) for x in operands))
    return pl.pallas_call(
        place,
        out_shape=(
            jax.ShapeDtypeStruct((1, PANEL, CH), BF16),
            jax.ShapeDtypeStruct((OWN, CH), F32),
        ),
        in_specs=[vmem] * 2,
        out_specs=(pl.BlockSpec(memory_space=pltpu.HBM),) * 2,
        scratch_shapes=[pltpu.SemaphoreType.DMA((2,))],
        compiler_params=pltpu.CompilerParams(vmem_limit_bytes=1024 * 1024),
    )(*grads)


def solution(mesh):
    placed = (P("dp", "seq", None), P("dp", "seq", None), P("seq", None), P())
    return jax.shard_map(
        on_device,
        mesh=mesh,
        in_specs=placed,
        out_specs=(P("dp", "seq", None), P(("seq", "dp"), None)),
        check_vma=False,
    )
```

```python
import functools
import math

import jax
import jax.numpy as jnp
import ml_dtypes
import numpy as np
from jax import lax
from jax.experimental import pallas as pl
from jax.experimental.pallas import tpu as pltpu
from jax.sharding import PartitionSpec as P

SEQ, ZED, CORES = 16, 16, 2
PANEL, HALF, CH, OWN = 256, 128, 128, 8
FREQ = PANEL
NEAR = 4
EARLY = ((0, 1), (1, 0), (4, 0), (1, 1), (4, 1), (0, 2), (0, 3), (8, 0), (8, 1), (12, 0), (12, 1), (2, 0), (2, 1), (5, 0), (5, 1), (3, 0), (3, 1))
COLUMNS = sorted({seq for seq, _ in EARLY})
SEQ_OFFSETS = sorted(
    ((i, j) for i in range(4) for j in range(4) if i + j), key=lambda o: -sum(min(k, 4 - k) for k in o)
)
Z_OFFSETS = sorted(range(1, ZED), key=lambda k: -min(k, ZED - k))
FAR, NEARER = Z_OFFSETS[:3], Z_OFFSETS[3:]
F32, BF16 = jnp.float32, jnp.bfloat16
NT = (((1,), (1,)), ((), ()))
NN = (((1,), (0,)), ((), ()))


def table():
    product = np.arange(PANEL)[:, None] * (2 * np.arange(FREQ)[None, :] + 1) % (4 * PANEL)
    phase = 2.0 * math.pi / (4 * PANEL) * product.astype(np.float64)
    full = np.concatenate([np.cos(phase), -np.sin(phase)], axis=1)
    high = full.astype(ml_dtypes.bfloat16)
    rest = (full - high.astype(np.float64)).astype(ml_dtypes.bfloat16)
    return np.stack([high, rest])


def dot(a, b, dims):
    return lax.dot_general(a, b, dims, preferred_element_type=F32)


def split(x):
    high = x.astype(BF16)
    return high, (x - high.astype(F32)).astype(BF16)


def correlate(x_of, g_ref, v_ref):
    for lane in range(0, FREQ, HALF):
        total_re = total_im = None
        for a in range(SEQ):
            x_re, x_im = x_of(a, lane)
            g_re = g_ref[a:, :, lane : lane + HALF]
            g_im = g_ref[a:, :, FREQ + lane : FREQ + lane + HALF]
            new_re = x_re * g_re + x_im * g_im
            new_im = x_re * g_im - x_im * g_re
            if a == 0:
                total_re, total_im = new_re, new_im
            else:
                n = SEQ - a
                total_re = jnp.concatenate([total_re[:n] + new_re, total_re[n:]], axis=0)
                total_im = jnp.concatenate([total_im[:n] + new_im, total_im[n:]], axis=0)
        for total, first in ((total_re, lane), (total_im, FREQ + lane)):
            high, rest = split(total.reshape(SEQ * OWN, HALF))
            v_ref[0 : SEQ * OWN, first : first + HALF] = high
            v_ref[SEQ * OWN :, first : first + HALF] = rest


def beside(dp, place):
    near = min((dp // CORES - place // CORES) % ZED, (place // CORES - dp // CORES) % ZED)
    return near == 0 or (near <= NEAR and dp % CORES == place % CORES)


def kernel(
    u_hbm, g_hbm, f_hbm, skip_hbm, w_hbm, in_ref, fg_ref,
    u_ref, g_ref, f_ref, skip_ref, w_ref, send_ug, recv_ug, send_f, recv_f, spec, spec_f, spin, v_ref, part, from_core, pair_sum, recv_z,
    own_sum, recv_s, send_in, recv_in, send_sem, recv_sem, load_sem, relay_sem, vouch_sem, pair_sem, recv_far, early_row, recv_early,
):
    me, dp = lax.axis_index("seq"), lax.axis_index("dp")
    z, core = lax.div(dp, CORES), lax.rem(dp, CORES)
    x, y = lax.div(me, 4), lax.rem(me, 4)
    seq_peers = [lax.rem(x + i, 4) * 4 + lax.rem(y + j, 4) for i, j in SEQ_OFFSETS]
    z_peer = lambda k: lax.rem(z + k, ZED)
    other = 1 - core

    loads = [
        pltpu.make_async_copy(src, dst, load_sem.at[i])
        for i, (src, dst) in enumerate(
            ((u_hbm, u_ref), (g_hbm, g_ref), (f_hbm, f_ref), (skip_hbm, skip_ref), (w_hbm, w_ref))
        )
    ]
    for load in loads[:2]:
        load.start()
    barrier = pltpu.get_barrier_semaphore()
    for k in Z_OFFSETS[-2 * NEAR :]:
        pl.semaphore_signal(barrier, inc=1, device_id={"dp": z_peer(k) * CORES + core})
    for peer in seq_peers:
        pl.semaphore_signal(barrier, inc=1, device_id={"seq": peer})
    pl.semaphore_signal(barrier, inc=1, device_id={"dp": z * CORES + other})

    for load in loads[2:]:
        load.start()

    any_of = lambda terms: functools.reduce(jnp.logical_or, terms)
    early = any_of([(me == seq) & (dp == place) for seq, place in EARLY])
    early_dp = any_of([dp == place for place in sorted({place for _, place in EARLY})])
    in_column = any_of([me == seq for seq in COLUMNS])
    greetings = SEQ + 2 * NEAR
    for seq, place in EARLY:
        strangers = [k for k in range(CORES * ZED) if not beside(k, place)]
        greetings += jnp.where((me == seq) & any_of([dp == k for k in strangers]), 1, 0)

        @pl.when((me == seq) & (dp == place))
        def _():
            for k in strangers:
                pl.semaphore_signal(barrier, inc=1, device_id={"dp": k})

    def send(src, dst, place, device):
        pltpu.make_async_remote_copy(
            src_ref=src, dst_ref=dst, send_sem=send_sem.at[place], recv_sem=recv_sem.at[place], device_id=device
        ).start()

    def await_bytes(ref, sem, place):
        pltpu.make_async_copy(ref, ref, sem.at[place]).wait()

    rows = lax.broadcasted_iota(jnp.int32, (CH, CH), 0)
    eye = (rows == lax.broadcasted_iota(jnp.int32, (CH, CH), 1)).astype(F32).astype(BF16)

    def stage(first, second, out_ref):
        first, second = dot(eye, first, NT), dot(eye, second, NT)
        for h in range(2):
            lanes = slice(h * HALF, (h + 1) * HALF)
            tile = jnp.concatenate(
                [first[:, lanes].reshape(SEQ, OWN, HALF), second[:, lanes].reshape(SEQ, OWN, HALF)], axis=1
            )
            out_ref[:, h] = tile.astype(BF16)

    loads[0].wait()
    loads[1].wait()
    stage(u_ref[0], g_ref[0], send_ug)
    loads[2].wait()
    loads[3].wait()
    tap = lax.broadcasted_iota(jnp.int32, (PANEL, CH), 0) + me
    filt = f_ref[...] + jnp.where(tap == 0, jnp.broadcast_to(skip_ref[...], (PANEL, CH)), 0.0)
    stage(*split(filt), send_f)

    pl.semaphore_wait(barrier, greetings)
    for k in (NEAR, ZED - NEAR):
        pl.semaphore_signal(relay_sem, inc=1, device_id={"dp": z_peer(k) * CORES + core})

    @pl.when(in_column)
    def _():
        for peer in seq_peers:
            pl.semaphore_signal(vouch_sem, inc=1, device_id={"seq": peer})

    for peer in seq_peers:
        send(send_ug.at[peer], recv_ug.at[me], 0, {"seq": peer})
    for peer in seq_peers:
        send(send_f.at[peer], recv_f.at[me], 1, {"seq": peer})
    recv_ug[me] = send_ug[me]
    recv_f[me] = send_f[me]

    loads[4].wait()
    pl.semaphore_wait(relay_sem, 2)
    pl.semaphore_signal(pair_sem, inc=1, device_id={"dp": z * CORES + other})

    pl.semaphore_wait(vouch_sem, jnp.where(in_column, len(COLUMNS) - 1, len(COLUMNS)))

    def transform(tiles_ref):
        lhs = jnp.concatenate(
            [tiles_ref[:, 0].reshape(2 * SEQ * OWN, HALF), tiles_ref[:, 1].reshape(2 * SEQ * OWN, HALF)], axis=1
        )
        return dot(lhs, w_ref[0], NN) + dot(lhs, w_ref[1], NN)

    await_bytes(recv_ug.at[pl.ds(0, SEQ - 1)], recv_sem, 0)
    spec[...] = transform(recv_ug).reshape(SEQ, 2, OWN, 2 * FREQ)

    lanes = lax.broadcasted_iota(jnp.int32, (OWN, FREQ), 1)
    sign = 1.0 - 2.0 * lax.rem(lanes, 2).astype(F32)
    for a in range(SEQ):
        re, im = spec[a, 1, :, :FREQ], spec[a, 1, :, FREQ:]
        if a < SEQ - 1:
            re, im = re + sign * spec[a + 1, 1, :, FREQ:], im - sign * spec[a + 1, 1, :, :FREQ]
        spin[a, :, :FREQ] = re
        spin[a, :, FREQ:] = im

    correlate(
        lambda a, lane: (
            spec[a, 0, :, lane : lane + HALF], spec[a, 0, :, FREQ + lane : FREQ + lane + HALF]
        ),
        spin, v_ref,
    )
    wide = dot(w_ref[0], v_ref[...], NT)
    weight = wide[:, :CH] + wide[:, CH:] + dot(w_ref[1], v_ref[0 : SEQ * OWN], NT)
    weight = weight * (1.0 / (PANEL * math.sqrt(CORES * ZED * SEQ * PANEL)))
    group = lax.div(lax.broadcasted_iota(jnp.int32, (2 * OWN, CH), 1), OWN)
    line = lax.broadcasted_iota(jnp.int32, (2 * OWN, CH), 0)

    def tell(i):
        seq, place = EARLY[i]
        turned = pltpu.roll(weight[place * OWN : (place + 1) * OWN], 0, 1, stride=OWN, stride_axis=0)
        place_of = lax.rem(line[:OWN] + seq, SEQ)
        row = jnp.sum(jnp.where(group[:OWN] == place_of, turned, 0.0), axis=0, keepdims=True)
        early_row[i : i + 1] = row
        here = (me == seq) & (dp == place)

        @pl.when(here)
        def _():
            recv_early[pl.ds(dp * SEQ + me, 1)] = row

        @pl.when(jnp.logical_not(here))
        def _():
            send(
                early_row.at[pl.ds(i, 1)], recv_early.at[pl.ds(dp * SEQ + me, 1)], 6,
                {"seq": seq, "dp": place},
            )

    tell(0)
    blocks = weight.reshape(ZED, CORES, OWN, CH)
    for side in range(CORES):
        part[side] = blocks[:, side]
    pl.semaphore_wait(pair_sem, 1)
    for i, k in enumerate(FAR):
        peer = z_peer(k)
        for side in range(CORES):
            send(part.at[side, peer], recv_far.at[i, core], 7, {"dp": peer * CORES + side})
    send(part.at[other], from_core, 2, {"dp": z * CORES + other})
    for i in range(1, len(EARLY)):
        tell(i)

    await_bytes(recv_f.at[pl.ds(0, SEQ - 1)], recv_sem, 1)
    both = transform(recv_f).reshape(SEQ, 2, OWN, 2 * FREQ)
    spec_f[...] = both[:, 0] + both[:, 1]

    await_bytes(from_core, recv_sem, 2)
    pair_sum[...] = part[core] + from_core[...]
    for i, k in enumerate(NEARER):
        peer = z_peer(k)
        send(pair_sum.at[peer], recv_z.at[i], 3, {"dp": peer * CORES + core})

    correlate(
        lambda a, lane: (spec_f[a, :, lane : lane + HALF], spec_f[a, :, FREQ + lane : FREQ + lane + HALF]),
        spin, v_ref,
    )
    tall = dot(v_ref[...], w_ref[0], NT)
    back = tall[: SEQ * OWN] + tall[SEQ * OWN :] + dot(v_ref[0 : SEQ * OWN], w_ref[1], NT)
    back = (back * (1.0 / PANEL)).reshape(SEQ, OWN, PANEL)
    send_in[...] = jnp.concatenate([back[:, :, :HALF], back[:, :, HALF:]], axis=1).astype(BF16)
    for peer in seq_peers:
        send(send_in.at[peer], recv_in.at[me], 4, {"seq": peer})
    recv_in[me] = send_in[me]

    await_bytes(recv_z, recv_sem, 3)
    await_bytes(recv_far, recv_sem, 7)
    far = recv_far[...].reshape(len(FAR) * CORES, OWN, CH)
    own_sum[...] = jnp.sum(recv_z[...], axis=0) + jnp.sum(far, axis=0) + pair_sum[z]
    @pl.when(early_dp)
    def _():
        for peer in seq_peers:
            direct = any_of([(peer == seq) & (dp == place) for seq, place in EARLY])

            @pl.when(jnp.logical_not(direct))
            def _():
                send(own_sum, recv_s.at[me], 5, {"seq": peer})

    @pl.when(jnp.logical_not(early_dp))
    def _():
        for peer in seq_peers:
            send(own_sum, recv_s.at[me], 5, {"seq": peer})

    recv_s[me] = own_sum[...]

    await_bytes(recv_in.at[pl.ds(0, SEQ - 1)], recv_sem, 4)
    for h in range(2):
        block = recv_in[...].astype(F32)[:, h * OWN : (h + 1) * OWN].reshape(CH, HALF)
        in_ref[0, h * HALF : (h + 1) * HALF] = block.T.astype(BF16)

    await_bytes(send_ug.at[pl.ds(0, SEQ - 1)], send_sem, 0)
    await_bytes(send_f.at[pl.ds(0, SEQ - 1)], send_sem, 1)
    await_bytes(from_core, send_sem, 2)
    await_bytes(recv_z, send_sem, 3)
    await_bytes(recv_far, send_sem, 7)
    await_bytes(send_in.at[pl.ds(0, SEQ - 1)], send_sem, 4)
    sent = SEQ - 1
    for seq, place in EARLY:
        sent -= jnp.where((dp == place) & (me != seq), 1, 0)

    def sent_one(i, carry):
        await_bytes(own_sum, send_sem, 5)
        return carry

    lax.fori_loop(0, sent, sent_one, 0)
    for seq, place in EARLY:
        @pl.when(jnp.logical_not((me == seq) & (dp == place)))
        def _():
            await_bytes(early_row.at[pl.ds(0, 1)], send_sem, 6)

    @pl.when(jnp.logical_not(early))
    def _():
        await_bytes(recv_s.at[pl.ds(0, SEQ - 1)], recv_sem, 5)
        result = jnp.zeros((OWN, CH), F32)
        for s in range(SEQ):
            turned = pltpu.roll(recv_s[s], lax.rem(s + SEQ - me, SEQ) * OWN, 1)
            result = jnp.where(group[:OWN] == s, turned, result)
        fg_ref[...] = result

    @pl.when(early)
    def _():
        await_bytes(recv_early.at[pl.ds(0, SEQ * CORES * ZED - 1)], recv_sem, 6)
        total = jnp.sum(recv_early[...].reshape(CORES * ZED, SEQ, CH), axis=0)
        total = pltpu.roll(total, (SEQ - me) * OWN, 1)
        turned = pltpu.roll(total, 0, 1, stride=OWN, stride_axis=0)
        for r in range(OWN):
            shifted = turned if r == 0 else pltpu.roll(turned, CH - r * OWN, 1)
            fg_ref[r : r + 1] = jnp.sum(jnp.where(group == line, shifted, 0.0), axis=0, keepdims=True)


def place(in_vmem, fg_vmem, in_hbm, fg_hbm, sem):
    copies = [
        pltpu.make_async_copy(in_vmem, in_hbm, sem.at[0]),
        pltpu.make_async_copy(fg_vmem, fg_hbm, sem.at[1]),
    ]
    for copy in copies:
        copy.start()
    for copy in copies:
        copy.wait()


def on_device(signal, out_grad, filt, skip):
    vmem = pl.BlockSpec(memory_space=pltpu.VMEM)
    operands = (signal, out_grad, filt, skip.reshape(1, CH), jnp.asarray(table()))
    tiles = (SEQ, 2, 2 * OWN, HALF)
    grads = pl.pallas_call(
        kernel,
        out_shape=(
            pltpu.VMEM((1, PANEL, CH), BF16),
            pltpu.VMEM((OWN, CH), F32),
        ),
        in_specs=[pl.BlockSpec(memory_space=pltpu.HBM)] * 5,
        out_specs=(vmem, vmem),
        scratch_shapes=[
            pltpu.VMEM((1, PANEL, CH), BF16),
            pltpu.VMEM((1, PANEL, CH), BF16),
            pltpu.VMEM((PANEL, CH), F32),
            pltpu.VMEM((1, CH), F32),
            pltpu.VMEM((2, PANEL, 2 * FREQ), BF16),
            pltpu.VMEM(tiles, BF16),
            pltpu.VMEM(tiles, BF16),
            pltpu.VMEM(tiles, BF16),
            pltpu.VMEM(tiles, BF16),
            pltpu.VMEM((SEQ, 2, OWN, 2 * FREQ), F32),
            pltpu.VMEM((SEQ, OWN, 2 * FREQ), F32),
            pltpu.VMEM((SEQ, OWN, 2 * FREQ), F32),
            pltpu.VMEM((2 * SEQ * OWN, 2 * FREQ), BF16),
            pltpu.VMEM((CORES, ZED, OWN, CH), F32),
            pltpu.VMEM((ZED, OWN, CH), F32),
            pltpu.VMEM((ZED, OWN, CH), F32),
            pltpu.VMEM((len(NEARER), OWN, CH), F32),
            pltpu.VMEM((OWN, CH), F32),
            pltpu.VMEM((SEQ, OWN, CH), F32),
            pltpu.VMEM((SEQ, 2 * OWN, HALF), BF16),
            pltpu.VMEM((SEQ, 2 * OWN, HALF), BF16),
            pltpu.SemaphoreType.DMA((8,)),
            pltpu.SemaphoreType.DMA((8,)),
            pltpu.SemaphoreType.DMA((5,)),
            pltpu.SemaphoreType.REGULAR,
            pltpu.SemaphoreType.REGULAR,
            pltpu.SemaphoreType.REGULAR,
            pltpu.VMEM((len(FAR), CORES, OWN, CH), F32),
            pltpu.VMEM((4 * OWN, CH), F32),
            pltpu.VMEM((SEQ * CORES * ZED, CH), F32),
        ],
        compiler_params=pltpu.CompilerParams(
            collective_id=0, has_side_effects=True, vmem_limit_bytes=16 * 1024 * 1024
        ),
    )(*(pltpu.with_memory_space_constraint(x, pltpu.HBM) for x in operands))
    return pl.pallas_call(
        place,
        out_shape=(
            jax.ShapeDtypeStruct((1, PANEL, CH), BF16),
            jax.ShapeDtypeStruct((OWN, CH), F32),
        ),
        in_specs=[vmem] * 2,
        out_specs=(pl.BlockSpec(memory_space=pltpu.HBM),) * 2,
        scratch_shapes=[pltpu.SemaphoreType.DMA((2,))],
        compiler_params=pltpu.CompilerParams(vmem_limit_bytes=1024 * 1024),
    )(*grads)


def solution(mesh):
    placed = (P("dp", "seq", None), P("dp", "seq", None), P("seq", None), P())
    return jax.shard_map(
        on_device,
        mesh=mesh,
        in_specs=placed,
        out_specs=(P("dp", "seq", None), P(("seq", "dp"), None)),
        check_vma=False,
    )
```

```python
import functools
import math

import jax
import jax.numpy as jnp
import ml_dtypes
import numpy as np
from jax import lax
from jax.experimental import pallas as pl
from jax.experimental.pallas import tpu as pltpu
from jax.sharding import PartitionSpec as P

SEQ, ZED, CORES = 16, 16, 2
PANEL, HALF, CH, OWN = 256, 128, 128, 8
FREQ = PANEL
NEAR = 4
EARLY = ((0, 1), (1, 0), (4, 0), (1, 1), (4, 1), (0, 2), (0, 3), (8, 0), (8, 1), (12, 0), (12, 1), (2, 0), (2, 1), (5, 0), (5, 1), (3, 0), (3, 1))
COLUMNS = sorted({seq for seq, _ in EARLY})
SEQ_OFFSETS = sorted(
    ((i, j) for i in range(4) for j in range(4) if i + j), key=lambda o: -sum(min(k, 4 - k) for k in o)
)
Z_OFFSETS = sorted(range(1, ZED), key=lambda k: -min(k, ZED - k))
FAR, NEARER = Z_OFFSETS[:3], Z_OFFSETS[3:]
F32, BF16 = jnp.float32, jnp.bfloat16
NT = (((1,), (1,)), ((), ()))
NN = (((1,), (0,)), ((), ()))


def table():
    product = np.arange(PANEL)[:, None] * (2 * np.arange(FREQ)[None, :] + 1) % (4 * PANEL)
    phase = 2.0 * math.pi / (4 * PANEL) * product.astype(np.float64)
    full = np.concatenate([np.cos(phase), -np.sin(phase)], axis=1)
    high = full.astype(ml_dtypes.bfloat16)
    rest = (full - high.astype(np.float64)).astype(ml_dtypes.bfloat16)
    return np.stack([high, rest])


def dot(a, b, dims):
    return lax.dot_general(a, b, dims, preferred_element_type=F32)


def split(x):
    high = x.astype(BF16)
    return high, (x - high.astype(F32)).astype(BF16)


def correlate(x_of, g_ref, v_ref):
    for lane in range(0, FREQ, HALF):
        total_re = total_im = None
        for a in range(SEQ):
            x_re, x_im = x_of(a, lane)
            g_re = g_ref[a:, :, lane : lane + HALF]
            g_im = g_ref[a:, :, FREQ + lane : FREQ + lane + HALF]
            new_re = x_re * g_re + x_im * g_im
            new_im = x_re * g_im - x_im * g_re
            if a == 0:
                total_re, total_im = new_re, new_im
            else:
                n = SEQ - a
                total_re = jnp.concatenate([total_re[:n] + new_re, total_re[n:]], axis=0)
                total_im = jnp.concatenate([total_im[:n] + new_im, total_im[n:]], axis=0)
        for total, first in ((total_re, lane), (total_im, FREQ + lane)):
            high, rest = split(total.reshape(SEQ * OWN, HALF))
            v_ref[0 : SEQ * OWN, first : first + HALF] = high
            v_ref[SEQ * OWN :, first : first + HALF] = rest


def beside(dp, place):
    near = min((dp // CORES - place // CORES) % ZED, (place // CORES - dp // CORES) % ZED)
    return near == 0 or (near <= NEAR and dp % CORES == place % CORES)


def kernel(
    u_hbm, g_hbm, f_hbm, skip_hbm, w_hbm, in_ref, fg_ref,
    u_ref, g_ref, f_ref, skip_ref, w_ref, send_ug, recv_ug, send_f, recv_f, spec, spec_f, spin, v_ref, part, from_core, pair_sum, recv_z,
    own_sum, recv_s, send_in, recv_in, send_sem, recv_sem, load_sem, relay_sem, vouch_sem, pair_sem, recv_far, early_row, recv_early,
):
    me, dp = lax.axis_index("seq"), lax.axis_index("dp")
    z, core = lax.div(dp, CORES), lax.rem(dp, CORES)
    x, y = lax.div(me, 4), lax.rem(me, 4)
    seq_peers = [lax.rem(x + i, 4) * 4 + lax.rem(y + j, 4) for i, j in SEQ_OFFSETS]
    z_peer = lambda k: lax.rem(z + k, ZED)
    other = 1 - core

    loads = [
        pltpu.make_async_copy(src, dst, load_sem.at[i])
        for i, (src, dst) in enumerate(
            ((u_hbm, u_ref), (g_hbm, g_ref), (f_hbm, f_ref), (skip_hbm, skip_ref), (w_hbm, w_ref))
        )
    ]
    barrier = pltpu.get_barrier_semaphore()
    for peer in seq_peers:
        pl.semaphore_signal(barrier, inc=1, device_id={"seq": peer})
    for k in Z_OFFSETS[-2 * NEAR :]:
        pl.semaphore_signal(barrier, inc=1, device_id={"dp": z_peer(k) * CORES + core})
    for load in loads[:2]:
        load.start()
    pl.semaphore_signal(barrier, inc=1, device_id={"dp": z * CORES + other})

    for load in loads[2:]:
        load.start()

    any_of = lambda terms: functools.reduce(jnp.logical_or, terms)
    early = any_of([(me == seq) & (dp == place) for seq, place in EARLY])
    early_dp = any_of([dp == place for place in sorted({place for _, place in EARLY})])
    in_column = any_of([me == seq for seq in COLUMNS])
    greetings = SEQ + 2 * NEAR
    for seq, place in EARLY:
        strangers = [k for k in range(CORES * ZED) if not beside(k, place)]
        greetings += jnp.where((me == seq) & any_of([dp == k for k in strangers]), 1, 0)

        @pl.when((me == seq) & (dp == place))
        def _():
            for k in strangers:
                pl.semaphore_signal(barrier, inc=1, device_id={"dp": k})

    def send(src, dst, place, device):
        pltpu.make_async_remote_copy(
            src_ref=src, dst_ref=dst, send_sem=send_sem.at[place], recv_sem=recv_sem.at[place], device_id=device
        ).start()

    def await_bytes(ref, sem, place):
        pltpu.make_async_copy(ref, ref, sem.at[place]).wait()

    rows = lax.broadcasted_iota(jnp.int32, (CH, CH), 0)
    eye = (rows == lax.broadcasted_iota(jnp.int32, (CH, CH), 1)).astype(F32).astype(BF16)

    def stage(first, second, out_ref):
        first, second = dot(eye, first, NT), dot(eye, second, NT)
        for h in range(2):
            lanes = slice(h * HALF, (h + 1) * HALF)
            tile = jnp.concatenate(
                [first[:, lanes].reshape(SEQ, OWN, HALF), second[:, lanes].reshape(SEQ, OWN, HALF)], axis=1
            )
            out_ref[:, h] = tile.astype(BF16)

    loads[0].wait()
    loads[1].wait()
    stage(u_ref[0], g_ref[0], send_ug)
    loads[2].wait()
    loads[3].wait()
    tap = lax.broadcasted_iota(jnp.int32, (PANEL, CH), 0) + me
    filt = f_ref[...] + jnp.where(tap == 0, jnp.broadcast_to(skip_ref[...], (PANEL, CH)), 0.0)
    stage(*split(filt), send_f)

    pl.semaphore_wait(barrier, greetings)
    for k in (NEAR, ZED - NEAR):
        pl.semaphore_signal(relay_sem, inc=1, device_id={"dp": z_peer(k) * CORES + core})

    @pl.when(in_column)
    def _():
        for peer in seq_peers:
            pl.semaphore_signal(vouch_sem, inc=1, device_id={"seq": peer})

    for peer in seq_peers:
        send(send_ug.at[peer], recv_ug.at[me], 0, {"seq": peer})
    for peer in seq_peers:
        send(send_f.at[peer], recv_f.at[me], 1, {"seq": peer})
    recv_ug[me] = send_ug[me]
    recv_f[me] = send_f[me]

    loads[4].wait()
    pl.semaphore_wait(relay_sem, 2)
    pl.semaphore_signal(pair_sem, inc=1, device_id={"dp": z * CORES + other})

    pl.semaphore_wait(vouch_sem, jnp.where(in_column, len(COLUMNS) - 1, len(COLUMNS)))

    def transform(tiles_ref):
        lhs = jnp.concatenate(
            [tiles_ref[:, 0].reshape(2 * SEQ * OWN, HALF), tiles_ref[:, 1].reshape(2 * SEQ * OWN, HALF)], axis=1
        )
        return dot(lhs, w_ref[0], NN) + dot(lhs, w_ref[1], NN)

    await_bytes(recv_ug.at[pl.ds(0, SEQ - 1)], recv_sem, 0)
    spec[...] = transform(recv_ug).reshape(SEQ, 2, OWN, 2 * FREQ)

    lanes = lax.broadcasted_iota(jnp.int32, (OWN, FREQ), 1)
    sign = 1.0 - 2.0 * lax.rem(lanes, 2).astype(F32)
    for a in range(SEQ):
        re, im = spec[a, 1, :, :FREQ], spec[a, 1, :, FREQ:]
        if a < SEQ - 1:
            re, im = re + sign * spec[a + 1, 1, :, FREQ:], im - sign * spec[a + 1, 1, :, :FREQ]
        spin[a, :, :FREQ] = re
        spin[a, :, FREQ:] = im

    correlate(
        lambda a, lane: (
            spec[a, 0, :, lane : lane + HALF], spec[a, 0, :, FREQ + lane : FREQ + lane + HALF]
        ),
        spin, v_ref,
    )
    wide = dot(w_ref[0], v_ref[...], NT)
    weight = wide[:, :CH] + wide[:, CH:] + dot(w_ref[1], v_ref[0 : SEQ * OWN], NT)
    weight = weight * (1.0 / (PANEL * math.sqrt(CORES * ZED * SEQ * PANEL)))
    group = lax.div(lax.broadcasted_iota(jnp.int32, (2 * OWN, CH), 1), OWN)
    line = lax.broadcasted_iota(jnp.int32, (2 * OWN, CH), 0)

    def tell(i):
        seq, place = EARLY[i]
        turned = pltpu.roll(weight[place * OWN : (place + 1) * OWN], 0, 1, stride=OWN, stride_axis=0)
        place_of = lax.rem(line[:OWN] + seq, SEQ)
        row = jnp.sum(jnp.where(group[:OWN] == place_of, turned, 0.0), axis=0, keepdims=True)
        early_row[i : i + 1] = row
        here = (me == seq) & (dp == place)

        @pl.when(here)
        def _():
            recv_early[pl.ds(dp * SEQ + me, 1)] = row

        @pl.when(jnp.logical_not(here))
        def _():
            send(
                early_row.at[pl.ds(i, 1)], recv_early.at[pl.ds(dp * SEQ + me, 1)], 6,
                {"seq": seq, "dp": place},
            )

    tell(0)
    blocks = weight.reshape(ZED, CORES, OWN, CH)
    for side in range(CORES):
        part[side] = blocks[:, side]
    pl.semaphore_wait(pair_sem, 1)
    for i, k in enumerate(FAR):
        peer = z_peer(k)
        for side in range(CORES):
            send(part.at[side, peer], recv_far.at[i, core], 7, {"dp": peer * CORES + side})
    send(part.at[other], from_core, 2, {"dp": z * CORES + other})
    for i in range(1, len(EARLY)):
        tell(i)

    await_bytes(recv_f.at[pl.ds(0, SEQ - 1)], recv_sem, 1)
    both = transform(recv_f).reshape(SEQ, 2, OWN, 2 * FREQ)
    spec_f[...] = both[:, 0] + both[:, 1]

    await_bytes(from_core, recv_sem, 2)
    pair_sum[...] = part[core] + from_core[...]
    for i, k in enumerate(NEARER):
        peer = z_peer(k)
        send(pair_sum.at[peer], recv_z.at[i], 3, {"dp": peer * CORES + core})

    correlate(
        lambda a, lane: (spec_f[a, :, lane : lane + HALF], spec_f[a, :, FREQ + lane : FREQ + lane + HALF]),
        spin, v_ref,
    )
    tall = dot(v_ref[...], w_ref[0], NT)
    back = tall[: SEQ * OWN] + tall[SEQ * OWN :] + dot(v_ref[0 : SEQ * OWN], w_ref[1], NT)
    back = (back * (1.0 / PANEL)).reshape(SEQ, OWN, PANEL)
    send_in[...] = jnp.concatenate([back[:, :, :HALF], back[:, :, HALF:]], axis=1).astype(BF16)
    for peer in seq_peers:
        send(send_in.at[peer], recv_in.at[me], 4, {"seq": peer})
    recv_in[me] = send_in[me]

    await_bytes(recv_z, recv_sem, 3)
    await_bytes(recv_far, recv_sem, 7)
    far = recv_far[...].reshape(len(FAR) * CORES, OWN, CH)
    own_sum[...] = jnp.sum(recv_z[...], axis=0) + jnp.sum(far, axis=0) + pair_sum[z]
    @pl.when(early_dp)
    def _():
        for peer in seq_peers:
            direct = any_of([(peer == seq) & (dp == place) for seq, place in EARLY])

            @pl.when(jnp.logical_not(direct))
            def _():
                send(own_sum, recv_s.at[me], 5, {"seq": peer})

    @pl.when(jnp.logical_not(early_dp))
    def _():
        for peer in seq_peers:
            send(own_sum, recv_s.at[me], 5, {"seq": peer})

    recv_s[me] = own_sum[...]

    await_bytes(recv_in.at[pl.ds(0, SEQ - 1)], recv_sem, 4)
    for h in range(2):
        block = recv_in[...].astype(F32)[:, h * OWN : (h + 1) * OWN].reshape(CH, HALF)
        in_ref[0, h * HALF : (h + 1) * HALF] = block.T.astype(BF16)

    await_bytes(send_ug.at[pl.ds(0, SEQ - 1)], send_sem, 0)
    await_bytes(send_f.at[pl.ds(0, SEQ - 1)], send_sem, 1)
    await_bytes(from_core, send_sem, 2)
    await_bytes(recv_z, send_sem, 3)
    await_bytes(recv_far, send_sem, 7)
    await_bytes(send_in.at[pl.ds(0, SEQ - 1)], send_sem, 4)
    sent = SEQ - 1
    for seq, place in EARLY:
        sent -= jnp.where((dp == place) & (me != seq), 1, 0)

    def sent_one(i, carry):
        await_bytes(own_sum, send_sem, 5)
        return carry

    lax.fori_loop(0, sent, sent_one, 0)
    for seq, place in EARLY:
        @pl.when(jnp.logical_not((me == seq) & (dp == place)))
        def _():
            await_bytes(early_row.at[pl.ds(0, 1)], send_sem, 6)

    @pl.when(jnp.logical_not(early))
    def _():
        await_bytes(recv_s.at[pl.ds(0, SEQ - 1)], recv_sem, 5)
        result = jnp.zeros((OWN, CH), F32)
        for s in range(SEQ):
            turned = pltpu.roll(recv_s[s], lax.rem(s + SEQ - me, SEQ) * OWN, 1)
            result = jnp.where(group[:OWN] == s, turned, result)
        fg_ref[...] = result

    @pl.when(early)
    def _():
        await_bytes(recv_early.at[pl.ds(0, SEQ * CORES * ZED - 1)], recv_sem, 6)
        total = jnp.sum(recv_early[...].reshape(CORES * ZED, SEQ, CH), axis=0)
        total = pltpu.roll(total, (SEQ - me) * OWN, 1)
        turned = pltpu.roll(total, 0, 1, stride=OWN, stride_axis=0)
        for r in range(OWN):
            shifted = turned if r == 0 else pltpu.roll(turned, CH - r * OWN, 1)
            fg_ref[r : r + 1] = jnp.sum(jnp.where(group == line, shifted, 0.0), axis=0, keepdims=True)


def place(in_vmem, fg_vmem, in_hbm, fg_hbm, sem):
    copies = [
        pltpu.make_async_copy(in_vmem, in_hbm, sem.at[0]),
        pltpu.make_async_copy(fg_vmem, fg_hbm, sem.at[1]),
    ]
    for copy in copies:
        copy.start()
    for copy in copies:
        copy.wait()


def on_device(signal, out_grad, filt, skip):
    vmem = pl.BlockSpec(memory_space=pltpu.VMEM)
    operands = (signal, out_grad, filt, skip.reshape(1, CH), jnp.asarray(table()))
    tiles = (SEQ, 2, 2 * OWN, HALF)
    grads = pl.pallas_call(
        kernel,
        out_shape=(
            pltpu.VMEM((1, PANEL, CH), BF16),
            pltpu.VMEM((OWN, CH), F32),
        ),
        in_specs=[pl.BlockSpec(memory_space=pltpu.HBM)] * 5,
        out_specs=(vmem, vmem),
        scratch_shapes=[
            pltpu.VMEM((1, PANEL, CH), BF16),
            pltpu.VMEM((1, PANEL, CH), BF16),
            pltpu.VMEM((PANEL, CH), F32),
            pltpu.VMEM((1, CH), F32),
            pltpu.VMEM((2, PANEL, 2 * FREQ), BF16),
            pltpu.VMEM(tiles, BF16),
            pltpu.VMEM(tiles, BF16),
            pltpu.VMEM(tiles, BF16),
            pltpu.VMEM(tiles, BF16),
            pltpu.VMEM((SEQ, 2, OWN, 2 * FREQ), F32),
            pltpu.VMEM((SEQ, OWN, 2 * FREQ), F32),
            pltpu.VMEM((SEQ, OWN, 2 * FREQ), F32),
            pltpu.VMEM((2 * SEQ * OWN, 2 * FREQ), BF16),
            pltpu.VMEM((CORES, ZED, OWN, CH), F32),
            pltpu.VMEM((ZED, OWN, CH), F32),
            pltpu.VMEM((ZED, OWN, CH), F32),
            pltpu.VMEM((len(NEARER), OWN, CH), F32),
            pltpu.VMEM((OWN, CH), F32),
            pltpu.VMEM((SEQ, OWN, CH), F32),
            pltpu.VMEM((SEQ, 2 * OWN, HALF), BF16),
            pltpu.VMEM((SEQ, 2 * OWN, HALF), BF16),
            pltpu.SemaphoreType.DMA((8,)),
            pltpu.SemaphoreType.DMA((8,)),
            pltpu.SemaphoreType.DMA((5,)),
            pltpu.SemaphoreType.REGULAR,
            pltpu.SemaphoreType.REGULAR,
            pltpu.SemaphoreType.REGULAR,
            pltpu.VMEM((len(FAR), CORES, OWN, CH), F32),
            pltpu.VMEM((4 * OWN, CH), F32),
            pltpu.VMEM((SEQ * CORES * ZED, CH), F32),
        ],
        compiler_params=pltpu.CompilerParams(
            collective_id=0, has_side_effects=True, vmem_limit_bytes=16 * 1024 * 1024
        ),
    )(*(pltpu.with_memory_space_constraint(x, pltpu.HBM) for x in operands))
    return pl.pallas_call(
        place,
        out_shape=(
            jax.ShapeDtypeStruct((1, PANEL, CH), BF16),
            jax.ShapeDtypeStruct((OWN, CH), F32),
        ),
        in_specs=[vmem] * 2,
        out_specs=(pl.BlockSpec(memory_space=pltpu.HBM),) * 2,
        scratch_shapes=[pltpu.SemaphoreType.DMA((2,))],
        compiler_params=pltpu.CompilerParams(vmem_limit_bytes=1024 * 1024),
    )(*grads)


def solution(mesh):
    placed = (P("dp", "seq", None), P("dp", "seq", None), P("seq", None), P())
    return jax.shard_map(
        on_device,
        mesh=mesh,
        in_specs=placed,
        out_specs=(P("dp", "seq", None), P(("seq", "dp"), None)),
        check_vma=False,
    )
```
